32 devices in a mesh: gx: 4 (over y, core), gy: 8 (over z, x).
Axes of the slice: x: 2, y: 2, z: 4, core: 2. Of those that a mesh axis runs over, the one named last changes fastest.
Arguments:
- pressure: float32 [256, 128, 512], P('gx', 'gy'), may hold values from -6 to 6
- divergence: float32 [256, 128, 512], P('gx', 'gy'), may hold values from -6 to 6
- diagonal: float32 [256, 128, 512], P('gx', 'gy'), may hold values from 0.05 to 0.5
- normals: float32 [3, 32768], P(None, ('gx', 'gy')), may hold values from -6 to 6
- traction: float32 [3, 32768], P(None, ('gx', 'gy')), may hold values from -3 to 3
- slot_of: int32 [4, 8192], P('gx'), may hold values from 0 to 24575, as said below
- counts: int32 [32], P(('gx', 'gy')), may hold values from 0 to 3072, as said below
- previous: float32 [3, 98304], P(None, ('gx', 'gy')), may hold values from -6 to 6
- secant_v: float32 [32, 3, 98304], P(None, None, ('gx', 'gy')), may hold values from -6 to 6
- secant_w: float32 [32, 3, 98304], P(None, None, ('gx', 'gy')), may hold values from -332.55374 to 332.55374
Outputs:
- pressure_new: float32 [256, 128, 512], P('gx', 'gy')
- coupled: float32 [3, 98304], P(None, ('gx', 'gy'))
The draws below stay inside these ranges and needn't reach their ends.
Inputs may be any that keep to these rules, and one draw needn't show every extreme that they name: Within each group (row of slot_of) the places are distinct; place o * 3072 + s has s < counts[a * 8 + o]; every such place is used; the rows of one device (aligned blocks of 1024 entries) send at most 384 rows to one owner, and exactly 384 to some owner. The counts of one group sum to 8192; some owner of every group holds exactly 3072.
All inputs are finite; a program needn't handle non-finite values.
Results may differ from the reference program's by a relative error of at most 0.00019.
Values sent between devices are 32-bit elements; how exact they have to be, the bound alone decides.
No kernel may reach another device: no remote copies, remote signals or barrier semaphores. Data moves between devices by JAX's collectives and lax.ppermute only.
A program may use at most 128 MiB of HBM per device.

```python
import math
import jax
import jax.numpy as jnp
from jax import lax

CX = 64
CY = 16
CZ = 512
SWEEPS = 2
K = 32
R_DEV = 1024
G_ROWS = 8192
NROWS = 32768
PAIR = 384
HEAVY = 1
CAP = 3072
OWN = 98304
NX = 256
NY = 128
N_GX = 4
N_GY = 8


def plan_group(group_key):
    first_key, second_key, third_key = jax.random.split(group_key, 3)
    owner_order = jax.random.permutation(first_key, N_GY)

    def one_source(source_key):
        position = jax.random.permutation(source_key, R_DEV)
        heavy_index = position // PAIR
        light_index = HEAVY + (position - HEAVY * PAIR) % (N_GY - HEAVY)
        chosen = jnp.where(position < HEAVY * PAIR, heavy_index, light_index)
        return owner_order[chosen]
    owners = jax.vmap(one_source)(jax.random.split(second_key, N_GY)).reshape(G_ROWS).astype(jnp.int32)
    tiebreak = jax.random.permutation(third_key, G_ROWS).astype(jnp.int32)
    score = owners * G_ROWS + tiebreak
    order = jnp.argsort(score, stable=True)
    owner_counts = jnp.sum((owners[:, None] == jnp.arange(N_GY, dtype=jnp.int32)[None, :]).astype(jnp.int32), axis=0)
    starts = jnp.cumsum(owner_counts) - owner_counts
    sorted_owner = owners[order]
    ranks = jnp.arange(G_ROWS, dtype=jnp.int32) - starts[sorted_owner]
    slots = jnp.zeros((G_ROWS,), jnp.int32).at[order].set(sorted_owner * CAP + ranks)
    return (slots, owner_counts)


def plan_all(key):
    base = jax.random.fold_in(key, 4711)
    group_keys = jax.vmap(lambda index: jax.random.fold_in(base, index))(jnp.arange(N_GX))
    return jax.vmap(plan_group)(group_keys)


def draw_slot_of(key, part):
    slots, owner_counts = plan_all(key)
    return slots


def draw_counts(key, part):
    slots, owner_counts = plan_all(key)
    return owner_counts.reshape(N_GX * N_GY)


def shard_levels(key, shape, cuts, low, high):
    gain, own = 1.0, jax.random.fold_in(key, 6)
    for dim, parts in cuts:
        heights = jnp.exp(jax.random.uniform(jax.random.fold_in(own, dim), (parts,), jnp.float32, low / len(cuts), high / len(cuts)))
        gain = gain * jnp.repeat(heights, shape[dim] // parts).reshape([-1 if axis == dim else 1 for axis in range(len(shape))])
    return gain


def noise(rng, shape, scale, reach, pieces=(), held_as=jnp.bfloat16):
    drawn = jax.random.normal(rng, shape, jnp.float32) * scale
    if len(pieces) > 0:
        drawn = shard_levels(rng, shape, pieces, -0.22, 0.18) * drawn
    return jnp.clip(drawn, min=-reach, max=reach).astype(held_as)


def setup_inputs(seed: int = 0) -> dict:
    streams_of = jax.random.split(jax.random.key(seed), 11)
    return {
        "pressure": noise(streams_of[0], (NX, NY, CZ), 1.0, 6.0, ((0, 4), (1, 8)), jnp.float32),
        "divergence": noise(streams_of[1], (NX, NY, CZ), 1.0, 6.0, ((0, 4), (1, 8)), jnp.float32),
        "diagonal": jnp.clip(jnp.exp(math.log(0.5) - 2.3025851 * jax.random.uniform(streams_of[2], (NX, NY, CZ), jnp.float32) ** shard_levels(streams_of[2], (NX, NY, CZ), ((0, 4), (1, 8)), -0.2, 0.2)), 0.05, 0.5),
        "normals": noise(streams_of[3], (3, NROWS), 1.0, 6.0, ((1, 32),), jnp.float32),
        "traction": noise(streams_of[4], (3, NROWS), 0.5, 3.0, ((1, 32),), jnp.float32),
        "slot_of": draw_slot_of(jax.random.fold_in(streams_of[10], 71), 0),
        "counts": draw_counts(jax.random.fold_in(streams_of[10], 71), 0),
        "previous": noise(streams_of[7], (3, OWN), 1.0, 6.0, ((1, 32),), jnp.float32),
        "secant_v": noise(streams_of[8], (K, 3, OWN), 1.0, 6.0, ((2, 32),), jnp.float32),
        "secant_w": noise(streams_of[9], (K, 3, OWN), ((3 * NROWS / K) ** 0.5), 332.55374, ((2, 32),), jnp.float32),
    }


def neighbours(field):
    padded = jnp.pad(field, 1)
    total = padded[2:, 1:-1, 1:-1] + padded[:-2, 1:-1, 1:-1]
    total = total + padded[1:-1, 2:, 1:-1] + padded[1:-1, :-2, 1:-1]
    total = total + padded[1:-1, 1:-1, 2:] + padded[1:-1, 1:-1, :-2]
    return total

def place_group(group_rows, group_slots):
    empty = jnp.zeros((3, N_GY * CAP), jnp.float32)
    return empty.at[:, group_slots].set(group_rows)

def reference(pressure, divergence, diagonal, normals, traction, slot_of, counts, previous, secant_v, secant_w):
    field = pressure
    for sweep_index in range(SWEEPS):
        field = (divergence + neighbours(field)) / (6.0 + diagonal)
    surface = field[:, :, CZ - 1].reshape(N_GX, CX, N_GY, CY).transpose(0, 2, 1, 3).reshape(NROWS)
    forces = normals * surface[None, :] + traction
    grouped = forces.reshape(3, N_GX, G_ROWS).transpose(1, 0, 2)
    owned = jax.vmap(place_group)(grouped, slot_of)
    owned = owned.reshape(N_GX, 3, N_GY * CAP).transpose(1, 0, 2).reshape(3, OWN)
    slot_index = jnp.arange(CAP, dtype=jnp.int32)
    occupied = (slot_index[None, :] < counts[:, None]).astype(jnp.float32).reshape(OWN)
    residual = occupied[None, :] * (owned - previous)
    masked_v = (secant_v * occupied[None, None, :]).reshape(K, 3 * OWN)
    gram = jnp.dot(masked_v, masked_v.T, precision=lax.Precision.HIGHEST)
    projection = jnp.dot(masked_v, residual.reshape(3 * OWN), precision=lax.Precision.HIGHEST)
    factor = jnp.linalg.cholesky(gram)
    coefficient = -jax.scipy.linalg.cho_solve((factor, True), projection)
    update = jnp.dot(coefficient, secant_w.reshape(K, 3 * OWN), precision=lax.Precision.HIGHEST).reshape(3, OWN)
    coupled = occupied[None, :] * (owned + update)
    return (field, coupled)
```

```python
import functools
import jax
import jax.numpy as jnp
from jax import lax
from jax.experimental import pallas as pl
from jax.experimental.pallas import tpu as pltpu
from jax.sharding import PartitionSpec as P

SWEEPS = 2
LANES = 128
F32 = jnp.float32
BF16 = jnp.bfloat16
VMEM = pl.BlockSpec(memory_space=pltpu.VMEM)
SMEM = pl.BlockSpec(memory_space=pltpu.SMEM)
HIGHEST = lax.Precision.HIGHEST


def pairs(count, parity):
    out = []
    for low in range(parity, count - 1, 2):
        out += [(low, low + 1), (low + 1, low)]
    return out


def swap(head, tail, axis):
    count = lax.axis_size(axis)
    even = lax.axis_index(axis) % 2 == 0
    first = lax.ppermute(jnp.where(even, tail, head), axis, pairs(count, 0))
    second = lax.ppermute(jnp.where(even, head, tail), axis, pairs(count, 1))
    return jnp.where(even, second, first), jnp.where(even, first, second)


def extended(cells, sides, width):
    for axis, dim in sides:
        head = lax.slice_in_dim(cells, 0, width, axis=dim)
        tail = lax.slice_in_dim(cells, cells.shape[dim] - width, cells.shape[dim], axis=dim)
        below, above = swap(head, tail, axis)
        cells = jnp.concatenate([below, cells, above], axis=dim)
    return cells


def stencil_sum(padded):
    padded = jnp.pad(padded, ((0, 0), (0, 0), (1, 1)))
    total = padded[2:, 1:-1, 1:-1] + padded[:-2, 1:-1, 1:-1]
    total = total + padded[1:-1, 2:, 1:-1] + padded[1:-1, :-2, 1:-1]
    total = total + padded[1:-1, 1:-1, 2:] + padded[1:-1, 1:-1, :-2]
    return total


def sweep_once(field, divergence, diagonal):
    padded = extended(field, (("gx", 0), ("gy", 1)), 1)
    return (divergence + stencil_sum(padded)) / (6.0 + diagonal)


def iota(shape, dim):
    return lax.broadcasted_iota(jnp.int32, shape, dim)


def occupied_rows(count, capacity):
    return (iota((1, capacity), 1) < count).astype(F32)


def gram_kernel(count_ref, v_ref, gram_ref):
    columns, capacity = v_ref.shape[1], v_ref.shape[2]
    occupied = occupied_rows(count_ref[0], capacity)
    total = jnp.zeros((columns, columns), F32)
    for c in range(v_ref.shape[0]):
        plain = v_ref[c]
        total += lax.dot_general(
            plain * occupied, plain, (((1,), (1,)), ((), ())), precision=HIGHEST, preferred_element_type=F32
        )
    rows = gram_ref.shape[0]
    gram_ref[...] = jnp.concatenate([total[j : j + rows] for j in range(0, columns, rows)], axis=1)


def gram_tile(counts, v):
    columns = v.shape[1]
    return pl.pallas_call(
        gram_kernel,
        out_shape=jax.ShapeDtypeStruct((columns * columns // LANES, LANES), F32),
        in_specs=[SMEM, VMEM],
        out_specs=VMEM,
        name="gram",
    )(counts, v)


def place_kernel(place_ref, count_ref, got_ref, slot_ref, previous_ref, v_ref, owned_ref, message_ref, gram_scratch):
    own = place_ref[0]
    sources, tiles = got_ref.shape[0], slot_ref.shape[0] // got_ref.shape[0]
    capacity = previous_ref.shape[1]
    high = capacity // LANES
    base = own * capacity

    def one_source(source, total):
        left, right = [], []
        for t in range(tiles):
            slots = slot_ref[pl.ds(source * tiles + t, 1), :]
            at_row = lax.shift_right_arithmetic(slots - base, 7) == iota((high, LANES), 0)
            right.append((jnp.bitwise_and(slots, LANES - 1) == iota((LANES, LANES), 0)).astype(F32))
            rough, fine = [], []
            for c in range(3):
                value = got_ref[source, pl.ds(c * tiles + t, 1), :]
                near = value.astype(BF16).astype(F32)
                rough.append(jnp.where(at_row, near, 0.0))
                fine.append(jnp.where(at_row, value - near, 0.0))
            left.append(jnp.concatenate(rough + fine, axis=0))
        left = jnp.concatenate(left, axis=1).astype(BF16)
        right = jnp.concatenate(right, axis=1).astype(BF16)
        return total + lax.dot_general(
            left, right, (((1,), (1,)), ((), ())), preferred_element_type=F32
        )

    total = lax.fori_loop(0, sources, one_source, jnp.zeros((6 * high, LANES), F32))
    owned = total[: 3 * high] + total[3 * high :]
    summed = jnp.zeros((v_ref.shape[1], LANES), F32)
    for c in range(3):
        for h in range(high):
            lanes = slice(h * LANES, (h + 1) * LANES)
            row = owned[c * high + h : c * high + h + 1]
            owned_ref[c : c + 1, lanes] = row
            held = iota((1, LANES), 1) + h * LANES < count_ref[0]
            residual = jnp.where(held, row - previous_ref[c : c + 1, lanes], 0.0)
            summed += v_ref[c, :, lanes] * residual
    projection = lax.dot_general(
        jnp.ones((8, LANES), F32), summed, (((1,), (1,)), ((), ())), precision=HIGHEST, preferred_element_type=F32
    )
    gram_rows = gram_scratch.shape[0]
    gram_scratch[...] = jnp.sum(got_ref[:, 3 * tiles : 3 * tiles + gram_rows, :], axis=0)
    chunk = gram_scratch[pl.ds(jnp.minimum(own, gram_rows - 1), 1), :]
    message_ref[:, :LANES] = jnp.where(own < gram_rows, chunk, 0.0)
    message_ref[:, LANES:] = jnp.concatenate(
        [projection[:1], jnp.zeros((1, LANES - projection.shape[1]), F32)], axis=1
    )


def place(own, counts, got, slots, previous, v):
    columns = v.shape[1]
    return pl.pallas_call(
        place_kernel,
        out_shape=(
            jax.ShapeDtypeStruct(previous.shape, F32),
            jax.ShapeDtypeStruct((1, 2 * LANES), F32),
        ),
        in_specs=[SMEM, SMEM, VMEM, VMEM, VMEM, VMEM],
        out_specs=(VMEM, VMEM),
        scratch_shapes=[pltpu.VMEM((columns * columns // LANES, LANES), F32)],
        name="place",
    )(own, counts, got, slots, previous, v)


def solve_kernel(groups, count_ref, got_ref, owned_ref, w_ref, coupled_ref):
    columns, capacity = w_ref.shape[1], w_ref.shape[2]
    gram_rows = columns * columns // LANES
    per_group = got_ref.shape[0] // groups
    tile = got_ref[:gram_rows, :LANES]
    for g in range(1, groups):
        tile += got_ref[g * per_group : g * per_group + gram_rows, :LANES]
    projection = jnp.sum(got_ref[:, LANES:], axis=0, keepdims=True)
    gram = jnp.concatenate([tile[:, j : j + columns] for j in range(0, LANES, columns)], axis=0)
    rows, lanes = iota((columns, LANES), 0), iota((columns, LANES), 1)
    right = jnp.sum(jnp.where(rows == lanes, projection, 0.0), axis=1, keepdims=True)
    system = jnp.concatenate([gram, jnp.zeros((columns, LANES - columns), F32)], axis=1)
    system = jnp.where(lanes == columns, right, system)
    for k in range(columns):
        pivot_row = system[k : k + 1] / system[k : k + 1, k : k + 1]
        system = jnp.where(rows == k, pivot_row, system - system[:, k : k + 1] * pivot_row)
    coefficient = -system[:, columns : columns + 1]
    for c in range(3):
        for h in range(capacity // LANES):
            at = slice(h * LANES, (h + 1) * LANES)
            update = jnp.sum(w_ref[c, :, at] * coefficient, axis=0, keepdims=True)
            held = iota((1, LANES), 1) + h * LANES < count_ref[0]
            coupled_ref[c : c + 1, at] = jnp.where(held, owned_ref[c : c + 1, at] + update, 0.0)


def solve(groups, counts, got, owned, w):
    return pl.pallas_call(
        functools.partial(solve_kernel, groups),
        out_shape=jax.ShapeDtypeStruct(owned.shape, F32),
        in_specs=[SMEM, VMEM, VMEM, VMEM],
        out_specs=VMEM,
        name="solve",
    )(counts, got, owned, w)


def exchanged(block, axes):
    count = lax.axis_size(axes)
    sent = jnp.broadcast_to(block[None], (count,) + block.shape)
    return lax.all_to_all(sent, axes, 0, 0, tiled=True)


def shards(
    pressure, divergence, diagonal, normals, traction, slot_of, counts, previous, secant_v, secant_w
):
    v = jnp.transpose(secant_v, (1, 0, 2))
    w = jnp.transpose(secant_w, (1, 0, 2))
    own = lax.axis_index("gy").astype(jnp.int32).reshape(1)
    gram = gram_tile(counts, v)
    field = pressure
    for sweep_index in range(SWEEPS):
        field = sweep_once(field, divergence, diagonal)
    surface = field[:, :, -1].reshape(-1)
    forces = normals * surface[None, :] + traction
    block = jnp.concatenate([forces.reshape(-1, LANES), gram], axis=0)
    got = exchanged(block, "gy")
    owned, message = place(own, counts, got, slot_of.reshape(-1, LANES), previous, v)
    shared = exchanged(message, ("gx", "gy")).reshape(-1, 2 * LANES)
    coupled = solve(lax.axis_size("gx"), counts, shared, owned, w)
    return (field, coupled)


def solution(mesh):
    placed = (
        P("gx", "gy", None),
        P("gx", "gy", None),
        P("gx", "gy", None),
        P(None, ("gx", "gy")),
        P(None, ("gx", "gy")),
        P("gx", None),
        P(("gx", "gy")),
        P(None, ("gx", "gy")),
        P(None, None, ("gx", "gy")),
        P(None, None, ("gx", "gy")),
    )
    return jax.shard_map(
        shards,
        mesh=mesh,
        in_specs=placed,
        out_specs=(P("gx", "gy", None), P(None, ("gx", "gy"))),
        check_vma=False,
    )
```

```python
import functools
import jax
import jax.numpy as jnp
from jax import lax
from jax.experimental import pallas as pl
from jax.experimental.pallas import tpu as pltpu
from jax.sharding import PartitionSpec as P

LANES = 128
F32 = jnp.float32
BF16 = jnp.bfloat16
VMEM = pl.BlockSpec(memory_space=pltpu.VMEM)
SMEM = pl.BlockSpec(memory_space=pltpu.SMEM)
HIGHEST = lax.Precision.HIGHEST


def pairs(count, parity):
    out = []
    for low in range(parity, count - 1, 2):
        out += [(low, low + 1), (low + 1, low)]
    return out


def swap(head, tail, axis):
    count = lax.axis_size(axis)
    even = lax.axis_index(axis) % 2 == 0
    first = lax.ppermute(jnp.where(even, tail, head), axis, pairs(count, 0))
    second = lax.ppermute(jnp.where(even, head, tail), axis, pairs(count, 1))
    return jnp.where(even, second, first), jnp.where(even, first, second)


def iota(shape, dim):
    return lax.broadcasted_iota(jnp.int32, shape, dim)


def occupied_rows(count, capacity):
    return (iota((1, capacity), 1) < count).astype(F32)


def gram_kernel(count_ref, v_ref, gram_ref):
    columns, capacity = v_ref.shape[1], v_ref.shape[2]
    occupied = occupied_rows(count_ref[0], capacity)
    total = jnp.zeros((columns, columns), F32)
    for c in range(v_ref.shape[0]):
        plain = v_ref[c]
        total += lax.dot_general(
            plain * occupied, plain, (((1,), (1,)), ((), ())), precision=HIGHEST, preferred_element_type=F32
        )
    rows = gram_ref.shape[0]
    gram_ref[...] = jnp.concatenate([total[j : j + rows] for j in range(0, columns, rows)], axis=1)


def gram_tile(counts, v):
    columns = v.shape[1]
    return pl.pallas_call(
        gram_kernel,
        out_shape=jax.ShapeDtypeStruct((columns * columns // LANES, LANES), F32),
        in_specs=[SMEM, VMEM],
        out_specs=VMEM,
        name="gram",
    )(counts, v)


def slab_kernel(pressure_ref, divergence_ref, diagonal_ref, planes_ref):
    cx, cy, width = pressure_ref.shape
    step = LANES // cy
    for k in range(cx // step):
        lanes = slice(k * LANES, (k + 1) * LANES)
        turned = [
            ref[k * step : (k + 1) * step].reshape(LANES, width).T
            for ref in (pressure_ref, divergence_ref, diagonal_ref)
        ]
        for row, (which, back) in enumerate(((0, 1), (0, 2), (0, 3), (1, 1), (1, 2), (2, 1), (2, 2))):
            line = turned[which][width - back : width - back + 1]
            planes_ref[row : row + 1, lanes] = 1.0 / (6.0 + line) if which == 2 else line
        planes_ref[7:8, lanes] = jnp.zeros((1, LANES), F32)


def slab(pressure, divergence, diagonal):
    cx, cy, cz = pressure.shape
    last = pl.BlockSpec((cx, cy, LANES), lambda i: (0, 0, cz // LANES - 1))
    return pl.pallas_call(
        slab_kernel,
        grid=(1,),
        out_shape=jax.ShapeDtypeStruct((8, cx * cy), F32),
        in_specs=[last, last, last],
        out_specs=pl.BlockSpec((8, cx * cy), lambda i: (0, 0)),
        name="slab",
    )(pressure, divergence, diagonal)


def rolled(block, shift, axis=1):
    return pltpu.roll(block, shift % block.shape[axis], axis)


def packed(parts, cy):
    place = lax.rem(iota(parts[0].shape, 1) + 2, cy) // 4
    out = parts[0]
    for k in range(1, 4):
        out = jnp.where(place == k, rolled(parts[k], 4 * k), out)
    return out


def surface_kernel(cy, planes_ref, below_ref, above_ref, normals_ref, traction_ref, gram_ref, out_ref, scratch):
    rows = planes_ref.shape[1]
    tiles = rows // LANES
    ext = jnp.concatenate([below_ref[...], planes_ref[...], above_ref[...]], axis=1)
    y = lax.rem(iota(ext.shape, 1), cy)

    def around(block):
        inner = jnp.where(y == 0, 0.0, rolled(block, 1)) + jnp.where(y == cy - 1, 0.0, rolled(block, -1))
        return rolled(block, cy) + rolled(block, -cy) + inner

    def line(row):
        return ext[row : row + 1]

    near = around(ext)
    once = (line(3) + near[0:1] + line(1)) * line(5)
    beneath = (line(4) + near[1:2] + line(0) + line(2)) * line(6)
    twice = (line(3) + around(jnp.broadcast_to(once, ext.shape))[0:1] + beneath) * line(5)
    surface = twice[:, LANES : LANES + rows]
    normals = normals_ref[...]
    forces = normals * surface + traction_ref[...]
    own = slice(LANES, LANES + rows)
    wide = lambda part: jnp.broadcast_to(part, (8, rows))
    first = packed(
        [wide(normals[0:1]), wide(normals[1:2]), wide(normals[2:3]), wide(line(0)[:, own])], cy
    )
    second = packed(
        [wide(part[:, own]) for part in (line(1), once, line(5), line(5) * line(6))], cy
    )
    for t in range(tiles):
        lanes = slice(t * LANES, (t + 1) * LANES)
        for c in range(3):
            scratch[c * tiles + t : c * tiles + t + 1] = forces[c : c + 1, lanes]
        scratch[3 * tiles + t : 3 * tiles + t + 1] = first[0:1, lanes]
        scratch[4 * tiles + t : 4 * tiles + t + 1] = second[0:1, lanes]
    low, high = ext[:, :LANES], ext[:, LANES + rows :]
    lane = iota((8, LANES), 1)
    side = jnp.where(
        lane < cy,
        rolled(low, cy)[0:1],
        jnp.where(
            lane < 2 * cy,
            rolled(high, cy)[0:1],
            jnp.where(lane < 3 * cy, rolled(low, 3 * cy)[5:6], rolled(high, 3 * cy)[5:6]),
        ),
    )
    scratch[5 * tiles : 5 * tiles + 8] = side
    scratch[5 * tiles + 8 :] = gram_ref[...]
    for d in range(out_ref.shape[0]):
        out_ref[d] = scratch[...]


def surface_message(count, cy, planes, below, above, normals, traction, gram):
    rows = 5 * planes.shape[1] // LANES + 8 + gram.shape[0]
    return pl.pallas_call(
        functools.partial(surface_kernel, cy),
        out_shape=jax.ShapeDtypeStruct((count, rows, LANES), F32),
        in_specs=[VMEM] * 6,
        out_specs=VMEM,
        scratch_shapes=[pltpu.VMEM((rows, LANES), F32)],
        name="surface",
    )(planes, below, above, normals, traction, gram)


def corrected(cy, got_ref, tiles, forces_ref):
    sources = got_ref.shape[0]
    rows = tiles * LANES

    def plane(index):
        return jnp.concatenate([got_ref[:, index * tiles + t, :] for t in range(tiles)], axis=1)

    def across(block):
        y, source = lax.rem(iota(block.shape, 1), cy), iota(block.shape, 0)
        before = rolled(rolled(block, 1, 0), 1 - cy)
        after = rolled(rolled(block, -1, 0), cy - 1)
        return jnp.where(
            (y == 0) & (source > 0), before, jnp.where((y == cy - 1) & (source < sources - 1), after, 0.0)
        )

    first, second = plane(3), plane(4)
    y = lax.rem(iota(first.shape, 1), cy)
    lane = iota(first.shape, 1)
    edge = lax.rem(y + 2, cy) < 4
    ratio = jnp.where(edge, rolled(second, -8), 0.0)
    both = jnp.where(edge, rolled(second, -12), 0.0)
    delta = ratio * across(rolled(first, -12))
    side = got_ref[:, 5 * tiles, :]
    side = rolled(side, -2 * cy) * across(side)
    end = jnp.concatenate([side] + [jnp.zeros_like(side)] * (tiles - 2) + [rolled(side, -2 * cy)], axis=1)
    total = jnp.where(lane < cy, end, rolled(delta, cy)) + jnp.where(lane >= rows - cy, end, rolled(delta, -cy))
    total += across(rolled(second, -4) + delta)
    total += jnp.where(y == 1, rolled(delta, 1), 0.0) + jnp.where(y == cy - 2, rolled(delta, -1), 0.0)
    change = ratio * total + both * across(second)
    for c in range(3):
        normal = jnp.where(edge, rolled(first, -4 * c), 0.0)
        forces = plane(c) + normal * change
        for t in range(tiles):
            forces_ref[c * tiles + t] = forces[:, t * LANES : (t + 1) * LANES]


def place_kernel(cy, place_ref, count_ref, got_ref, slot_ref, previous_ref, v_ref, owned_ref, message_ref, gram_scratch, forces_ref):
    own = place_ref[0]
    sources, tiles = got_ref.shape[0], slot_ref.shape[0] // got_ref.shape[0]
    capacity = previous_ref.shape[1]
    high = capacity // LANES
    base = own * capacity
    corrected(cy, got_ref, tiles, forces_ref)

    def one_source(source, total):
        left, right = [], []
        for t in range(tiles):
            slots = slot_ref[pl.ds(source * tiles + t, 1), :]
            at_row = lax.shift_right_arithmetic(slots - base, 7) == iota((high, LANES), 0)
            right.append((jnp.bitwise_and(slots, LANES - 1) == iota((LANES, LANES), 0)).astype(F32))
            rough, fine = [], []
            for c in range(3):
                value = forces_ref[c * tiles + t, pl.ds(source, 1), :]
                near = value.astype(BF16).astype(F32)
                rough.append(jnp.where(at_row, near, 0.0))
                fine.append(jnp.where(at_row, value - near, 0.0))
            left.append(jnp.concatenate(rough + fine, axis=0))
        left = jnp.concatenate(left, axis=1).astype(BF16)
        right = jnp.concatenate(right, axis=1).astype(BF16)
        return total + lax.dot_general(
            left, right, (((1,), (1,)), ((), ())), preferred_element_type=F32
        )

    total = lax.fori_loop(0, sources, one_source, jnp.zeros((6 * high, LANES), F32))
    owned = total[: 3 * high] + total[3 * high :]
    summed = jnp.zeros((v_ref.shape[1], LANES), F32)
    for c in range(3):
        for h in range(high):
            lanes = slice(h * LANES, (h + 1) * LANES)
            row = owned[c * high + h : c * high + h + 1]
            owned_ref[c : c + 1, lanes] = row
            held = iota((1, LANES), 1) + h * LANES < count_ref[0]
            residual = jnp.where(held, row - previous_ref[c : c + 1, lanes], 0.0)
            summed += v_ref[c, :, lanes] * residual
    projection = lax.dot_general(
        jnp.ones((8, LANES), F32), summed, (((1,), (1,)), ((), ())), precision=HIGHEST, preferred_element_type=F32
    )
    gram_rows = gram_scratch.shape[0]
    gram_scratch[...] = jnp.sum(got_ref[:, 5 * tiles + 8 :, :], axis=0)
    chunk = gram_scratch[pl.ds(jnp.minimum(own, gram_rows - 1), 1), :]
    message = jnp.concatenate(
        [
            jnp.where(own < gram_rows, chunk, 0.0),
            projection[:1],
            jnp.zeros((1, LANES - projection.shape[1]), F32),
        ],
        axis=1,
    )
    message_ref[...] = jnp.broadcast_to(message, message_ref.shape)


def place(devices, cy, own, counts, got, slots, previous, v):
    columns = v.shape[1]
    return pl.pallas_call(
        functools.partial(place_kernel, cy),
        out_shape=(
            jax.ShapeDtypeStruct(previous.shape, F32),
            jax.ShapeDtypeStruct((devices, 2 * LANES), F32),
        ),
        in_specs=[SMEM, SMEM, VMEM, VMEM, VMEM, VMEM],
        out_specs=(VMEM, VMEM),
        scratch_shapes=[
            pltpu.VMEM((columns * columns // LANES, LANES), F32),
            pltpu.VMEM((3 * slots.shape[0] // got.shape[0], got.shape[0], LANES), F32),
        ],
        name="place",
    )(own, counts, got, slots, previous, v)


def solve_kernel(groups, count_ref, got_ref, owned_ref, w_ref, coupled_ref):
    columns, capacity = w_ref.shape[1], w_ref.shape[2]
    gram_rows = columns * columns // LANES
    per_group = got_ref.shape[0] // groups
    tile = got_ref[:gram_rows, :LANES]
    for g in range(1, groups):
        tile += got_ref[g * per_group : g * per_group + gram_rows, :LANES]
    projection = jnp.sum(got_ref[:, LANES:], axis=0, keepdims=True)
    gram = jnp.concatenate([tile[:, j : j + columns] for j in range(0, LANES, columns)], axis=0)
    rows, lanes = iota((columns, LANES), 0), iota((columns, LANES), 1)
    right = jnp.sum(jnp.where(rows == lanes, projection, 0.0), axis=1, keepdims=True)
    system = jnp.concatenate([gram, jnp.zeros((columns, LANES - columns), F32)], axis=1)
    system = jnp.where(lanes == columns, right, system)
    for k in range(columns):
        pivot_row = system[k : k + 1] / system[k : k + 1, k : k + 1]
        system = jnp.where(rows == k, pivot_row, system - system[:, k : k + 1] * pivot_row)
    coefficient = -system[:, columns : columns + 1]
    for c in range(3):
        for h in range(capacity // LANES):
            at = slice(h * LANES, (h + 1) * LANES)
            update = jnp.sum(w_ref[c, :, at] * coefficient, axis=0, keepdims=True)
            held = iota((1, LANES), 1) + h * LANES < count_ref[0]
            coupled_ref[c : c + 1, at] = jnp.where(held, owned_ref[c : c + 1, at] + update, 0.0)


def solve(groups, counts, got, owned, w):
    return pl.pallas_call(
        functools.partial(solve_kernel, groups),
        out_shape=jax.ShapeDtypeStruct(owned.shape, F32),
        in_specs=[SMEM, VMEM, VMEM, VMEM],
        out_specs=VMEM,
        name="solve",
    )(counts, got, owned, w)


BIG = pltpu.CompilerParams(vmem_limit_bytes=40 * 1024 * 1024)


def shifted(here, low, high):
    y, z = iota(here.shape, 0), iota(here.shape, 1)
    before = jnp.where(y == 0, low, rolled(here, 1, 0))
    after = jnp.where(y == here.shape[0] - 1, high, rolled(here, -1, 0))
    left = jnp.where(z == 0, 0.0, rolled(here, 1))
    right = jnp.where(z == here.shape[1] - 1, 0.0, rolled(here, -1))
    return before + after + left + right


def first_kernel(p_ref, d_ref, g_ref, below_ref, above_ref, once_ref, ratio_ref, low_ref, high_ref):
    cx, cy = p_ref.shape[0], p_ref.shape[1]

    def sweep(before, here, after, source, ratio):
        return (source + before + after + shifted(here, 0.0, 0.0)) * ratio

    once_ref[0] = sweep(below_ref[1], below_ref[0], p_ref[0], below_ref[2], below_ref[3])
    once_ref[cx + 1] = sweep(above_ref[1], above_ref[0], p_ref[cx - 1], above_ref[2], above_ref[3])

    def step(x, carry):
        before, here = carry
        after = jnp.where(x == cx - 1, above_ref[0], p_ref[jnp.minimum(x + 1, cx - 1)])
        ratio = 1.0 / (6.0 + g_ref[x])
        ratio_ref[x] = ratio
        once_ref[x + 1] = sweep(before, here, after, d_ref[x], ratio)
        return here, after

    lax.fori_loop(0, cx, step, (below_ref[0], p_ref[0]), unroll=4)
    for out_ref, y in ((low_ref, 0), (high_ref, cy - 1)):
        out_ref[:cx] = p_ref[:, y, :]
        out_ref[cx : 2 * cx] = once_ref[1 : cx + 1, y, :]
        out_ref[2 * cx : 3 * cx] = ratio_ref[:, y, :]
        ends = [ref[row, y : y + 1, :] for ref, row in ((below_ref, 0), (above_ref, 0), (below_ref, 3), (above_ref, 3))]
        out_ref[3 * cx :] = jnp.concatenate(ends + [jnp.zeros((4, p_ref.shape[2]), F32)], axis=0)


def first_sweep(p, d, g, below, above):
    cx, cy, cz = p.shape
    face = jax.ShapeDtypeStruct((3 * cx + 8, cz), F32)
    return pl.pallas_call(
        first_kernel,
        out_shape=(jax.ShapeDtypeStruct((cx + 2, cy, cz), F32), jax.ShapeDtypeStruct(p.shape, F32), face, face),
        in_specs=[VMEM] * 5,
        out_specs=(VMEM,) * 4,
        compiler_params=BIG,
        name="first_sweep",
    )(p, d, g, below, above)


def second_kernel(once_ref, ratio_ref, d_ref, low_ref, high_ref, below_ref, above_ref, out_ref, rows_ref):
    cx, cy, cz = out_ref.shape
    corners = 3 * cx
    for side, (own_ref, far_ref) in enumerate(((low_ref, below_ref), (high_ref, above_ref))):
        rows_ref[side] = far_ref[cx : 2 * cx] + far_ref[2 * cx : 3 * cx] * own_ref[:cx]
        lacking = own_ref[2 * cx : 3 * cx] * far_ref[:cx]
        last = own_ref[corners + 3 : corners + 4] * far_ref[corners + 1 : corners + 2]
        rows_ref[2 + side] = jnp.concatenate([lacking[1:], last], axis=0)
    y = iota((cy, cz), 0)

    def completed(plane, low, high):
        return plane + jnp.where(y == 0, low, jnp.where(y == cy - 1, high, 0.0))

    def owed(row, far_row):
        return [
            own_ref[row : row + 1] * far_ref[far_row : far_row + 1]
            for own_ref, far_ref in ((low_ref, below_ref), (high_ref, above_ref))
        ]

    def chunk(c, carry):
        before, here = carry
        rows = [rows_ref[k, pl.ds(8 * c, 8), :] for k in range(4)]
        for j in range(8):
            x = 8 * c + j
            low, high, low_next, high_next = [block[j : j + 1] for block in rows]
            after = completed(once_ref[x + 2], low_next, high_next)
            out_ref[x] = (d_ref[x] + before + after + shifted(here, low, high)) * ratio_ref[x]
            before, here = here, after
        return before, here

    start = (
        completed(once_ref[0], *owed(corners + 2, corners)),
        completed(once_ref[1], *owed(2 * cx, 0)),
    )
    lax.fori_loop(0, cx // 8, chunk, start)


def second_sweep(once, ratio, d, low, high, below, above):
    cx, cy, cz = d.shape
    return pl.pallas_call(
        second_kernel,
        out_shape=jax.ShapeDtypeStruct(d.shape, F32),
        in_specs=[VMEM] * 7,
        out_specs=VMEM,
        scratch_shapes=[pltpu.VMEM((4, cx, cz), F32)],
        compiler_params=BIG,
        name="second_sweep",
    )(once, ratio, d, low, high, below, above)


def shards(
    pressure, divergence, diagonal, normals, traction, slot_of, counts, previous, secant_v, secant_w
):
    groups, owners = lax.axis_size("gx"), lax.axis_size("gy")
    cy = pressure.shape[1]
    v = jnp.transpose(secant_v, (1, 0, 2))
    w = jnp.transpose(secant_w, (1, 0, 2))
    own = lax.axis_index("gy").astype(jnp.int32).reshape(1)
    planes = slab(pressure, divergence, diagonal)
    below, above = swap(planes[:, :LANES], planes[:, -LANES:], "gx")
    gram = gram_tile(counts, v)
    block = surface_message(owners, cy, planes, below, above, normals, traction, gram)
    got = lax.all_to_all(block, "gy", 0, 0, tiled=True)
    owned, message = place(
        groups * owners, cy, own, counts, got, slot_of.reshape(-1, LANES), previous, v
    )
    shared = lax.all_to_all(message, ("gx", "gy"), 0, 0, tiled=True)
    coupled = solve(groups, counts, shared, owned, w)
    head = jnp.concatenate([pressure[:2], divergence[:1], 1.0 / (6.0 + diagonal[:1])])
    tail = jnp.concatenate([pressure[-1:], pressure[-2:-1], divergence[-1:], 1.0 / (6.0 + diagonal[-1:])])
    left, right = swap(head, tail, "gx")
    once, ratio, low, high = first_sweep(pressure, divergence, diagonal, left, right)
    beneath, beyond = swap(low, high, "gy")
    field = second_sweep(once, ratio, divergence, low, high, beneath, beyond)
    return (field, coupled)


def solution(mesh):
    placed = (
        P("gx", "gy", None),
        P("gx", "gy", None),
        P("gx", "gy", None),
        P(None, ("gx", "gy")),
        P(None, ("gx", "gy")),
        P("gx", None),
        P(("gx", "gy")),
        P(None, ("gx", "gy")),
        P(None, None, ("gx", "gy")),
        P(None, None, ("gx", "gy")),
    )
    return jax.shard_map(
        shards,
        mesh=mesh,
        in_specs=placed,
        out_specs=(P("gx", "gy", None), P(None, ("gx", "gy"))),
        check_vma=False,
    )
```

```python
import functools
import jax
import jax.numpy as jnp
from jax import lax
from jax.experimental import pallas as pl
from jax.experimental.pallas import tpu as pltpu
from jax.sharding import PartitionSpec as P

LANES = 128
F32 = jnp.float32
BF16 = jnp.bfloat16
VMEM = pl.BlockSpec(memory_space=pltpu.VMEM)
ANY = pl.BlockSpec(memory_space=pl.ANY)
SMEM = pl.BlockSpec(memory_space=pltpu.SMEM)
HIGHEST = lax.Precision.HIGHEST


def pairs(count, parity):
    out = []
    for low in range(parity, count - 1, 2):
        out += [(low, low + 1), (low + 1, low)]
    return out


def traded(first, second, axis):
    count = lax.axis_size(axis)
    return lax.ppermute(first, axis, pairs(count, 0)), lax.ppermute(second, axis, pairs(count, 1))


def iota(shape, dim):
    return lax.broadcasted_iota(jnp.int32, shape, dim)


def occupied_rows(count, capacity):
    return (iota((1, capacity), 1) < count).astype(F32)


def gram_kernel(count_ref, v_ref, gram_ref):
    columns, capacity = v_ref.shape[1], v_ref.shape[2]
    occupied = occupied_rows(count_ref[0], capacity)
    total = jnp.zeros((columns, columns), F32)
    for c in range(v_ref.shape[0]):
        plain = v_ref[c]
        total += lax.dot_general(
            plain * occupied, plain, (((1,), (1,)), ((), ())), precision=HIGHEST, preferred_element_type=F32
        )
    rows = gram_ref.shape[0]
    gram_ref[...] = jnp.concatenate([total[j : j + rows] for j in range(0, columns, rows)], axis=1)


def gram_tile(counts, v):
    columns = v.shape[1]
    return pl.pallas_call(
        gram_kernel,
        out_shape=jax.ShapeDtypeStruct((columns * columns // LANES, LANES), F32),
        in_specs=[SMEM, VMEM],
        out_specs=VMEM,
        compiler_params=limit(8),
        name="gram",
    )(counts, v)


def slab_kernel(
    even_x_ref, even_y_ref, p_ref, d_ref, g_ref, planes_ref, first_ref, second_ref, y_first_ref, y_second_ref,
    held, ratios, tile_sems, face_sems, y_sems,
):
    cx, cy, cz = p_ref.shape
    step = LANES // cy
    half = cx // 2
    even, even_y = even_x_ref[0] == 1, even_y_ref[0] == 1
    fetches = []
    for part in range(2):
        for which, ref in enumerate((p_ref, d_ref, g_ref)):
            at = pl.ds(part * half, half)
            fetches.append(
                pltpu.make_async_copy(
                    ref.at[at, :, pl.ds(cz - LANES, LANES)], held.at[which, at], tile_sems.at[part, which]
                )
            )
    for fetch in fetches:
        fetch.start()

    def face(out_ref, side, sources):
        return [
            pltpu.make_async_copy(
                ref.at[plane],
                ratios.at[side] if k == 3 else out_ref.at[pl.ds(k * cy, cy)],
                face_sems.at[side, k],
            )
            for k, (ref, plane) in enumerate(sources)
        ]

    head = ((p_ref, 0), (p_ref, 1), (d_ref, 0), (g_ref, 0))
    tail = ((p_ref, cx - 1), (p_ref, cx - 2), (d_ref, cx - 1), (g_ref, cx - 1))

    @pl.when(even)
    def _():
        for copy in face(second_ref, 0, head) + face(first_ref, 1, tail):
            copy.start()

    @pl.when(~even)
    def _():
        for copy in face(first_ref, 0, head) + face(second_ref, 1, tail):
            copy.start()

    def edge(out_ref, y, at):
        return pltpu.make_async_copy(p_ref.at[:, y, :], out_ref, y_sems.at[at])

    @pl.when(even_y)
    def _():
        edge(y_first_ref, cy - 1, 0).start()
        edge(y_second_ref, 0, 1).start()

    @pl.when(~even_y)
    def _():
        edge(y_first_ref, 0, 0).start()
        edge(y_second_ref, cy - 1, 1).start()

    planes_ref[7:8] = jnp.zeros((1, cx * cy), F32)
    for part in range(2):
        for fetch in fetches[3 * part : 3 * part + 3]:
            fetch.wait()
        for k in range(part * half // step, (part + 1) * half // step):
            lanes = slice(k * LANES, (k + 1) * LANES)
            turned = [held[which, k * step : (k + 1) * step].reshape(LANES, LANES).T for which in range(3)]
            for row, (which, back) in enumerate(((0, 1), (0, 2), (0, 3), (1, 1), (1, 2), (2, 1), (2, 2))):
                line = turned[which][LANES - back : LANES - back + 1]
                planes_ref[row : row + 1, lanes] = 1.0 / (6.0 + line) if which == 2 else line
    for copy in face(first_ref, 0, head) + face(first_ref, 1, tail):
        copy.wait()
    edge(y_first_ref, 0, 0).wait()
    edge(y_second_ref, 0, 1).wait()
    low, high = 1.0 / (6.0 + ratios[0]), 1.0 / (6.0 + ratios[1])
    own_low, own_high = planes_ref[:, :LANES], planes_ref[:, cx * cy - LANES :]
    for out_ref, above in ((first_ref, even), (second_ref, ~even)):
        out_ref[3 * cy : 4 * cy] = jnp.where(above, high, low)
        out_ref[4 * cy :] = jnp.zeros((8, cz), F32)
        out_ref[4 * cy :, :LANES] = jnp.where(above, own_high, own_low)


def in_hbm(array):
    return pltpu.with_memory_space_constraint(array, pltpu.HBM)


def limit(mib):
    return pltpu.CompilerParams(vmem_limit_bytes=mib * 1024 * 1024)


def slab(even_x, even_y, p, d, g):
    cx, cy, cz = p.shape
    face = jax.ShapeDtypeStruct((4 * cy + 8, cz), F32)
    edge = jax.ShapeDtypeStruct((cx, cz), F32)
    return pl.pallas_call(
        slab_kernel,
        out_shape=(jax.ShapeDtypeStruct((8, cx * cy), F32), face, face, edge, edge),
        in_specs=[SMEM, SMEM] + [ANY] * 3,
        out_specs=(VMEM,) * 5,
        scratch_shapes=[
            pltpu.VMEM((3, cx, cy, LANES), F32),
            pltpu.VMEM((2, cy, cz), F32),
            pltpu.SemaphoreType.DMA((2, 3)),
            pltpu.SemaphoreType.DMA((2, 4)),
            pltpu.SemaphoreType.DMA((2,)),
        ],
        compiler_params=limit(8),
        name="slab",
    )(even_x, even_y, in_hbm(p), in_hbm(d), in_hbm(g))


def rolled(block, shift, axis=1):
    return pltpu.roll(block, shift % block.shape[axis], axis)


def packed(parts, cy):
    place = lax.rem(iota(parts[0].shape, 1) + 2, cy) // 4
    out = parts[0]
    for k in range(1, 4):
        out = jnp.where(place == k, rolled(parts[k], 4 * k), out)
    return out


def surface_kernel(cy, even_ref, planes_ref, first_ref, second_ref, normals_ref, traction_ref, gram_ref, out_ref, scratch):
    rows = planes_ref.shape[1]
    tiles = rows // LANES
    first, second = first_ref[4 * cy :, :LANES], second_ref[4 * cy :, :LANES]
    even = even_ref[0] == 1
    ext = jnp.concatenate(
        [jnp.where(even, second, first), planes_ref[...], jnp.where(even, first, second)], axis=1
    )
    y = lax.rem(iota(ext.shape, 1), cy)

    def around(block):
        inner = jnp.where(y == 0, 0.0, rolled(block, 1)) + jnp.where(y == cy - 1, 0.0, rolled(block, -1))
        return rolled(block, cy) + rolled(block, -cy) + inner

    def line(row):
        return ext[row : row + 1]

    near = around(ext)
    once = (line(3) + near[0:1] + line(1)) * line(5)
    beneath = (line(4) + near[1:2] + line(0) + line(2)) * line(6)
    twice = (line(3) + around(jnp.broadcast_to(once, ext.shape))[0:1] + beneath) * line(5)
    surface = twice[:, LANES : LANES + rows]
    normals = normals_ref[...]
    forces = normals * surface + traction_ref[...]
    own = slice(LANES, LANES + rows)
    wide = lambda part: jnp.broadcast_to(part, (8, rows))
    first = packed(
        [wide(normals[0:1]), wide(normals[1:2]), wide(normals[2:3]), wide(line(0)[:, own])], cy
    )
    second = packed(
        [wide(part[:, own]) for part in (line(1), once, line(5), line(5) * line(6))], cy
    )
    for t in range(tiles):
        lanes = slice(t * LANES, (t + 1) * LANES)
        for c in range(3):
            scratch[c * tiles + t : c * tiles + t + 1] = forces[c : c + 1, lanes]
        scratch[3 * tiles + t : 3 * tiles + t + 1] = first[0:1, lanes]
        scratch[4 * tiles + t : 4 * tiles + t + 1] = second[0:1, lanes]
    low, high = ext[:, :LANES], ext[:, LANES + rows :]
    lane = iota((8, LANES), 1)
    side = jnp.where(
        lane < cy,
        rolled(low, cy)[0:1],
        jnp.where(
            lane < 2 * cy,
            rolled(high, cy)[0:1],
            jnp.where(lane < 3 * cy, rolled(low, 3 * cy)[5:6], rolled(high, 3 * cy)[5:6]),
        ),
    )
    scratch[5 * tiles : 5 * tiles + 8] = side
    scratch[5 * tiles + 8 :] = gram_ref[...]
    for d in range(out_ref.shape[0]):
        out_ref[d] = scratch[...]


def surface_message(count, cy, even, planes, first, second, normals, traction, gram):
    rows = 5 * planes.shape[1] // LANES + 8 + gram.shape[0]
    return pl.pallas_call(
        functools.partial(surface_kernel, cy),
        out_shape=jax.ShapeDtypeStruct((count, rows, LANES), F32),
        in_specs=[SMEM] + [VMEM] * 6,
        out_specs=VMEM,
        scratch_shapes=[pltpu.VMEM((rows, LANES), F32)],
        compiler_params=limit(8),
        name="surface",
    )(even, planes, first, second, normals, traction, gram)


def corrected(cy, got_ref, tiles, forces_ref):
    sources = got_ref.shape[0]
    rows = tiles * LANES

    def plane(index):
        return jnp.concatenate([got_ref[:, index * tiles + t, :] for t in range(tiles)], axis=1)

    def across(block):
        y, source = lax.rem(iota(block.shape, 1), cy), iota(block.shape, 0)
        before = rolled(rolled(block, 1, 0), 1 - cy)
        after = rolled(rolled(block, -1, 0), cy - 1)
        return jnp.where(
            (y == 0) & (source > 0), before, jnp.where((y == cy - 1) & (source < sources - 1), after, 0.0)
        )

    first, second = plane(3), plane(4)
    y = lax.rem(iota(first.shape, 1), cy)
    lane = iota(first.shape, 1)
    edge = lax.rem(y + 2, cy) < 4
    ratio = jnp.where(edge, rolled(second, -8), 0.0)
    both = jnp.where(edge, rolled(second, -12), 0.0)
    delta = ratio * across(rolled(first, -12))
    side = got_ref[:, 5 * tiles, :]
    side = rolled(side, -2 * cy) * across(side)
    end = jnp.concatenate([side] + [jnp.zeros_like(side)] * (tiles - 2) + [rolled(side, -2 * cy)], axis=1)
    total = jnp.where(lane < cy, end, rolled(delta, cy)) + jnp.where(lane >= rows - cy, end, rolled(delta, -cy))
    total += across(rolled(second, -4) + delta)
    total += jnp.where(y == 1, rolled(delta, 1), 0.0) + jnp.where(y == cy - 2, rolled(delta, -1), 0.0)
    change = ratio * total + both * across(second)
    for c in range(3):
        normal = jnp.where(edge, rolled(first, -4 * c), 0.0)
        forces = plane(c) + normal * change
        for t in range(tiles):
            forces_ref[c * tiles + t] = forces[:, t * LANES : (t + 1) * LANES]


def place_kernel(cy, place_ref, count_ref, got_ref, slot_ref, previous_ref, v_ref, owned_ref, message_ref, gram_scratch, forces_ref, held_v, arrived):
    own = place_ref[0]
    sources, tiles = got_ref.shape[0], slot_ref.shape[0] // got_ref.shape[0]
    capacity = previous_ref.shape[1]
    high = capacity // LANES
    base = own * capacity
    fetch = pltpu.make_async_copy(v_ref, held_v, arrived)
    fetch.start()
    corrected(cy, got_ref, tiles, forces_ref)

    def one_source(source, total):
        left, right = [], []
        for t in range(tiles):
            slots = slot_ref[pl.ds(source * tiles + t, 1), :]
            at_row = lax.shift_right_arithmetic(slots - base, 7) == iota((high, LANES), 0)
            right.append((jnp.bitwise_and(slots, LANES - 1) == iota((LANES, LANES), 0)).astype(F32))
            rough, fine = [], []
            for c in range(3):
                value = forces_ref[c * tiles + t, pl.ds(source, 1), :]
                near = value.astype(BF16).astype(F32)
                rough.append(jnp.where(at_row, near, 0.0))
                fine.append(jnp.where(at_row, value - near, 0.0))
            left.append(jnp.concatenate(rough + fine, axis=0))
        left = jnp.concatenate(left, axis=1).astype(BF16)
        right = jnp.concatenate(right, axis=1).astype(BF16)
        return total + lax.dot_general(
            left, right, (((1,), (1,)), ((), ())), preferred_element_type=F32
        )

    total = lax.fori_loop(0, sources, one_source, jnp.zeros((6 * high, LANES), F32))
    owned = total[: 3 * high] + total[3 * high :]
    fetch.wait()
    summed = jnp.zeros((v_ref.shape[1], LANES), F32)
    for c in range(3):
        for h in range(high):
            lanes = slice(h * LANES, (h + 1) * LANES)
            row = owned[c * high + h : c * high + h + 1]
            owned_ref[c : c + 1, lanes] = row
            held = iota((1, LANES), 1) + h * LANES < count_ref[0]
            residual = jnp.where(held, row - previous_ref[c : c + 1, lanes], 0.0)
            summed += held_v[c, :, lanes] * residual
    projection = lax.dot_general(
        jnp.ones((8, LANES), F32), summed, (((1,), (1,)), ((), ())), precision=HIGHEST, preferred_element_type=F32
    )
    gram_rows = gram_scratch.shape[0]
    gram_scratch[...] = jnp.sum(got_ref[:, 5 * tiles + 8 :, :], axis=0)
    chunk = gram_scratch[pl.ds(jnp.minimum(own, gram_rows - 1), 1), :]
    message = jnp.concatenate(
        [
            jnp.where(own < gram_rows, chunk, 0.0),
            projection[:1],
            jnp.zeros((1, LANES - projection.shape[1]), F32),
        ],
        axis=1,
    )
    message_ref[...] = jnp.broadcast_to(message[None], message_ref.shape)


def place(devices, cy, own, counts, got, slots, previous, v):
    columns = v.shape[1]
    return pl.pallas_call(
        functools.partial(place_kernel, cy),
        out_shape=(
            jax.ShapeDtypeStruct(previous.shape, F32),
            jax.ShapeDtypeStruct((devices, 1, 2 * LANES), F32),
        ),
        in_specs=[SMEM, SMEM, VMEM, VMEM, VMEM, ANY],
        out_specs=(VMEM, VMEM),
        scratch_shapes=[
            pltpu.VMEM((columns * columns // LANES, LANES), F32),
            pltpu.VMEM((3 * slots.shape[0] // got.shape[0], got.shape[0], LANES), F32),
            pltpu.VMEM(v.shape, F32),
            pltpu.SemaphoreType.DMA,
        ],
        compiler_params=limit(12),
        name="place",
    )(own, counts, got, slots, previous, v)


def solve_kernel(groups, count_ref, got_ref, owned_ref, w_ref, coupled_ref, held_w, arrived):
    fetch = pltpu.make_async_copy(w_ref, held_w, arrived)
    fetch.start()
    columns, capacity = w_ref.shape[1], w_ref.shape[2]
    gram_rows = columns * columns // LANES
    per_group = got_ref.shape[0] // groups
    tile = got_ref[:gram_rows, 0, :LANES]
    for g in range(1, groups):
        tile += got_ref[g * per_group : g * per_group + gram_rows, 0, :LANES]
    projection = jnp.sum(got_ref[:, 0, LANES:], axis=0, keepdims=True)
    gram = jnp.concatenate([tile[:, j : j + columns] for j in range(0, LANES, columns)], axis=0)
    rows, lanes = iota((columns, LANES), 0), iota((columns, LANES), 1)
    right = jnp.sum(jnp.where(rows == lanes, projection, 0.0), axis=1, keepdims=True)
    system = jnp.concatenate([gram, jnp.zeros((columns, LANES - columns), F32)], axis=1)
    system = jnp.where(lanes == columns, right, system)
    for k in range(columns):
        pivot_row = system[k : k + 1] / system[k : k + 1, k : k + 1]
        system = jnp.where(rows == k, pivot_row, system - system[:, k : k + 1] * pivot_row)
    coefficient = -system[:, columns : columns + 1]
    fetch.wait()
    for c in range(3):
        for h in range(capacity // LANES):
            at = slice(h * LANES, (h + 1) * LANES)
            update = jnp.sum(held_w[c, :, at] * coefficient, axis=0, keepdims=True)
            held = iota((1, LANES), 1) + h * LANES < count_ref[0]
            coupled_ref[c : c + 1, at] = jnp.where(held, owned_ref[c : c + 1, at] + update, 0.0)


def solve(groups, counts, got, owned, w):
    return pl.pallas_call(
        functools.partial(solve_kernel, groups),
        out_shape=jax.ShapeDtypeStruct(owned.shape, F32),
        in_specs=[SMEM, VMEM, VMEM, ANY],
        out_specs=VMEM,
        scratch_shapes=[pltpu.VMEM(w.shape, F32), pltpu.SemaphoreType.DMA],
        compiler_params=limit(8),
        name="solve",
    )(counts, got, owned, w)


def shifted(here, low, high):
    y, z = iota(here.shape, 0), iota(here.shape, 1)
    before = jnp.where(y == 0, low, rolled(here, 1, 0))
    after = jnp.where(y == here.shape[0] - 1, high, rolled(here, -1, 0))
    left = jnp.where(z == 0, 0.0, rolled(here, 1))
    right = jnp.where(z == here.shape[1] - 1, 0.0, rolled(here, -1))
    return before + after + left + right


CHUNK = 8


def halo_plane(even, first_ref, second_ref, k, above, cy):
    rows = slice(k * cy, (k + 1) * cy)
    return jnp.where(even != above, second_ref[rows], first_ref[rows])


def edge_kernel(
    even_x_ref, even_y_ref, p_ref, d_ref, g_ref, first_ref, second_ref, y_first_ref, y_second_ref,
    to_first_ref, to_second_ref, held, sems,
):
    cx, cy, cz = p_ref.shape
    columns = [(p_ref, 0), (p_ref, 1), (d_ref, 0), (g_ref, 0), (p_ref, cy - 1), (p_ref, cy - 2), (d_ref, cy - 1), (g_ref, cy - 1)]
    fetches = [
        pltpu.make_async_copy(ref.at[:, y, :], held.at[k], sems.at[k]) for k, (ref, y) in enumerate(columns)
    ]
    for fetch in fetches:
        fetch.start()
    for fetch in fetches:
        fetch.wait()
    even_x, even_y = even_x_ref[0] == 1, even_y_ref[0] == 1
    x, z = iota((cx, cz), 0), iota((cx, cz), 1)
    rows = []
    for side, y in enumerate((0, cy - 1)):
        here, inner, source, diagonal = [held[4 * side + k] for k in range(4)]
        below = halo_plane(even_x, first_ref, second_ref, 0, False, cy)[y : y + 1]
        above = halo_plane(even_x, first_ref, second_ref, 0, True, cy)[y : y + 1]
        total = source + inner + jnp.where(even_y != (side == 1), y_second_ref[...], y_first_ref[...])
        total += jnp.where(x == 0, below, rolled(here, 1, 0)) + jnp.where(x == cx - 1, above, rolled(here, -1, 0))
        total += jnp.where(z == 0, 0.0, rolled(here, 1)) + jnp.where(z == cz - 1, 0.0, rolled(here, -1))
        once = total * (1.0 / (6.0 + diagonal))
        rows.append((once, jnp.concatenate([below, above, jnp.zeros((6, cz), F32)], axis=0)))
    for at, k in ((slice(0, cx), 0), (slice(cx, cx + 8), 1)):
        to_first_ref[at] = jnp.where(even_y, rows[1][k], rows[0][k])
        to_second_ref[at] = jnp.where(even_y, rows[0][k], rows[1][k])


def swept_edges(even_x, even_y, p, d, g, first, second, y_first, y_second):
    cx, cy, cz = p.shape
    out = jax.ShapeDtypeStruct((cx + 8, cz), F32)
    return pl.pallas_call(
        edge_kernel,
        out_shape=(out, out),
        in_specs=[SMEM, SMEM] + [ANY] * 3 + [VMEM] * 4,
        out_specs=(VMEM, VMEM),
        scratch_shapes=[pltpu.VMEM((8, cx, cz), F32), pltpu.SemaphoreType.DMA((8,))],
        compiler_params=limit(8),
        name="edges",
    )(even_x, even_y, in_hbm(p), in_hbm(d), in_hbm(g), first, second, y_first, y_second)


def sweeps_kernel(
    even_x_ref, even_y_ref, p_ref, d_ref, g_ref, first_ref, second_ref, y_first_ref, y_second_ref,
    far_first_ref, far_second_ref, out_ref, held_p, held_d, held_g, once_ref, rows_ref, in_sems, out_sems,
):
    cx, cy, cz = p_ref.shape
    steps = cx // CHUNK
    even_x, even_y = even_x_ref[0] == 1, even_y_ref[0] == 1

    def arrive(at):
        planes = pl.ds(at * CHUNK, CHUNK)
        return [
            pltpu.make_async_copy(ref.at[planes], held.at[planes], in_sems.at[k, at])
            for k, (ref, held) in enumerate(((p_ref, held_p), (d_ref, held_d), (g_ref, held_g)))
        ]

    def leave(at):
        planes = pl.ds(at * CHUNK, CHUNK)
        return pltpu.make_async_copy(held_p.at[planes], out_ref.at[planes], out_sems.at[at])

    for at in range(steps):
        for copy in arrive(at):
            copy.start()
    for k, (one, two) in enumerate(((y_first_ref, y_second_ref), (far_first_ref, far_second_ref))):
        rows_ref[2 * k, : one.shape[0]] = jnp.where(even_y, two[...], one[...])
        rows_ref[2 * k + 1, : one.shape[0]] = jnp.where(even_y, one[...], two[...])
    halo = lambda k, above: halo_plane(even_x, first_ref, second_ref, k, above, cy)

    def sweep(before, here, after, source, ratio, low, high):
        return (source + before + after + shifted(here, low, high)) * ratio

    def rows(k, at):
        return [rows_ref[2 * k + side, pl.ds(pl.multiple_of(at * CHUNK, CHUNK), CHUNK), :] for side in range(2)]

    for copy in arrive(0):
        copy.wait()

    def first_chunk(at, carry):
        @pl.when(at + 1 < steps)
        def _():
            for copy in arrive(jnp.minimum(at + 1, steps - 1)):
                copy.wait()

        before, here = carry
        lows, highs = rows(0, at)
        for j in range(CHUNK):
            x = at * CHUNK + j
            after = held_p[jnp.minimum(x + 1, cx - 1)]
            if j == CHUNK - 1:
                after = jnp.where(x == cx - 1, halo(0, True), after)
            ratio = 1.0 / (6.0 + held_g[x])
            once_ref[x] = sweep(before, here, after, held_d[x], ratio, lows[j : j + 1], highs[j : j + 1])
            held_g[x] = ratio
            before, here = here, after
        return before, here

    lax.fori_loop(0, steps, first_chunk, (halo(0, False), held_p[0]))
    ends = [rows_ref[2 + side, cx : cx + 8] for side in range(2)]
    start = sweep(
        halo(1, False), halo(0, False), held_p[0], halo(2, False), halo(3, False), ends[0][:1], ends[1][:1]
    )
    once_ref[cx] = sweep(
        held_p[cx - 1], halo(0, True), halo(1, True), halo(2, True), halo(3, True), ends[0][1:2], ends[1][1:2]
    )

    def second_chunk(at, carry):
        before, here = carry
        lows, highs = rows(1, at)
        for j in range(CHUNK):
            x = at * CHUNK + j
            after = once_ref[x + 1]
            held_p[x] = sweep(before, here, after, held_d[x], held_g[x], lows[j : j + 1], highs[j : j + 1])
            before, here = here, after
        leave(at).start()
        return before, here

    lax.fori_loop(0, steps, second_chunk, (start, once_ref[0]))
    for at in range(steps):
        leave(at).wait()


def both_sweeps(even_x, even_y, p, d, g, *beside):
    cx, cy, cz = p.shape
    return pl.pallas_call(
        sweeps_kernel,
        out_shape=jax.ShapeDtypeStruct(p.shape, F32),
        in_specs=[SMEM, SMEM] + [ANY] * 3 + [VMEM] * 6,
        out_specs=ANY,
        scratch_shapes=[pltpu.VMEM(p.shape, F32)] * 3
        + [
            pltpu.VMEM((cx + 1, cy, cz), F32),
            pltpu.VMEM((4, cx + 8, cz), F32),
            pltpu.SemaphoreType.DMA((3, cx // CHUNK)),
            pltpu.SemaphoreType.DMA((cx // CHUNK,)),
        ],
        compiler_params=limit(20),
        name="sweeps",
    )(even_x, even_y, in_hbm(p), in_hbm(d), in_hbm(g), *beside)


def shards(
    pressure, divergence, diagonal, normals, traction, slot_of, counts, previous, secant_v, secant_w
):
    groups, owners = lax.axis_size("gx"), lax.axis_size("gy")
    cy = pressure.shape[1]
    v = jnp.transpose(secant_v, (1, 0, 2))
    w = jnp.transpose(secant_w, (1, 0, 2))
    own = lax.axis_index("gy").astype(jnp.int32).reshape(1)
    even_x, even_y = [(1 - lax.axis_index(axis) % 2).astype(jnp.int32).reshape(1) for axis in ("gx", "gy")]
    fluid = (even_x, even_y, pressure, divergence, diagonal)
    planes, first, second, y_first, y_second = slab(*fluid)
    faces = traded(first, second, "gx")
    y_edges = traded(y_first, y_second, "gy")
    faces, y_edges = lax.optimization_barrier((faces, y_edges))
    gram = gram_tile(counts, v)
    block = surface_message(owners, cy, even_x, planes, *faces, normals, traction, gram)
    got = lax.all_to_all(block, "gy", 0, 0, tiled=True)
    far_edges = traded(*swept_edges(*fluid, *faces, *y_edges), "gy")
    owned, message = place(
        groups * owners, cy, own, counts, got, slot_of.reshape(-1, LANES), previous, v
    )
    shared = lax.all_to_all(message, ("gx", "gy"), 0, 0, tiled=True)
    field = both_sweeps(*fluid, *faces, *y_edges, *far_edges)
    coupled = solve(groups, counts, shared, owned, w)
    return (field, coupled)


def solution(mesh):
    placed = (
        P("gx", "gy", None),
        P("gx", "gy", None),
        P("gx", "gy", None),
        P(None, ("gx", "gy")),
        P(None, ("gx", "gy")),
        P("gx", None),
        P(("gx", "gy")),
        P(None, ("gx", "gy")),
        P(None, None, ("gx", "gy")),
        P(None, None, ("gx", "gy")),
    )
    return jax.shard_map(
        shards,
        mesh=mesh,
        in_specs=placed,
        out_specs=(P("gx", "gy", None), P(None, ("gx", "gy"))),
        check_vma=False,
    )
```

```python
import functools
import jax
import jax.numpy as jnp
from jax import lax
from jax.experimental import pallas as pl
from jax.experimental.pallas import tpu as pltpu
from jax.sharding import PartitionSpec as P

LANES = 128
F32 = jnp.float32
BF16 = jnp.bfloat16
VMEM = pl.BlockSpec(memory_space=pltpu.VMEM)
ANY = pl.BlockSpec(memory_space=pl.ANY)
SMEM = pl.BlockSpec(memory_space=pltpu.SMEM)
HIGHEST = lax.Precision.HIGHEST


def pairs(count, parity):
    out = []
    for low in range(parity, count - 1, 2):
        out += [(low, low + 1), (low + 1, low)]
    return out


def traded(first, second, axis):
    count = lax.axis_size(axis)
    return lax.ppermute(first, axis, pairs(count, 0)), lax.ppermute(second, axis, pairs(count, 1))


def iota(shape, dim):
    return lax.broadcasted_iota(jnp.int32, shape, dim)


def occupied_rows(count, capacity):
    return (iota((1, capacity), 1) < count).astype(F32)


def gram_kernel(count_ref, v_ref, gram_ref):
    columns, capacity = v_ref.shape[1], v_ref.shape[2]
    occupied = occupied_rows(count_ref[0], capacity)
    total = jnp.zeros((columns, columns), F32)
    for c in range(v_ref.shape[0]):
        plain = v_ref[c]
        total += lax.dot_general(
            plain * occupied, plain, (((1,), (1,)), ((), ())), precision=HIGHEST, preferred_element_type=F32
        )
    rows = gram_ref.shape[0]
    gram_ref[...] = jnp.concatenate([total[j : j + rows] for j in range(0, columns, rows)], axis=1)


def gram_tile(counts, v):
    columns = v.shape[1]
    return pl.pallas_call(
        gram_kernel,
        out_shape=jax.ShapeDtypeStruct((columns * columns // LANES, LANES), F32),
        in_specs=[SMEM, VMEM],
        out_specs=VMEM,
        compiler_params=limit(8),
        name="gram",
    )(counts, v)


def faces_kernel(
    even_x_ref, even_y_ref, p_ref, d_ref, g_ref, first_ref, second_ref, y_first_ref, y_second_ref,
    ratios, face_sems, y_sems,
):
    cx, cy, cz = p_ref.shape
    even_x, even_y = even_x_ref[0] == 1, even_y_ref[0] == 1

    def face(out_ref, side, sources):
        return [
            pltpu.make_async_copy(
                ref.at[plane],
                ratios.at[side] if k == 3 else out_ref.at[pl.ds(k * cy, cy)],
                face_sems.at[side, k],
            )
            for k, (ref, plane) in enumerate(sources)
        ]

    def edge(out_ref, y, at):
        return pltpu.make_async_copy(p_ref.at[:, y, :], out_ref, y_sems.at[at])

    head = ((p_ref, 0), (p_ref, 1), (d_ref, 0), (g_ref, 0))
    tail = ((p_ref, cx - 1), (p_ref, cx - 2), (d_ref, cx - 1), (g_ref, cx - 1))

    @pl.when(even_x)
    def _():
        for copy in face(second_ref, 0, head) + face(first_ref, 1, tail):
            copy.start()

    @pl.when(~even_x)
    def _():
        for copy in face(first_ref, 0, head) + face(second_ref, 1, tail):
            copy.start()

    @pl.when(even_y)
    def _():
        edge(y_first_ref, cy - 1, 0).start()
        edge(y_second_ref, 0, 1).start()

    @pl.when(~even_y)
    def _():
        edge(y_first_ref, 0, 0).start()
        edge(y_second_ref, cy - 1, 1).start()

    for copy in face(first_ref, 0, head) + face(first_ref, 1, tail):
        copy.wait()
    low, high = 1.0 / (6.0 + ratios[0]), 1.0 / (6.0 + ratios[1])
    for out_ref, above in ((first_ref, even_x), (second_ref, ~even_x)):
        out_ref[3 * cy :] = jnp.where(above, high, low)
    edge(y_first_ref, 0, 0).wait()
    edge(y_second_ref, 0, 1).wait()


def outer_faces(even_x, even_y, p, d, g):
    cx, cy, cz = p.shape
    face = jax.ShapeDtypeStruct((4 * cy, cz), F32)
    edge = jax.ShapeDtypeStruct((cx, cz), F32)
    return pl.pallas_call(
        faces_kernel,
        out_shape=(face, face, edge, edge),
        in_specs=[SMEM, SMEM] + [ANY] * 3,
        out_specs=(VMEM,) * 4,
        scratch_shapes=[
            pltpu.VMEM((2, cy, cz), F32),
            pltpu.SemaphoreType.DMA((2, 4)),
            pltpu.SemaphoreType.DMA((2,)),
        ],
        compiler_params=limit(8),
        name="faces",
    )(even_x, even_y, in_hbm(p), in_hbm(d), in_hbm(g))


def slab_kernel(p_ref, d_ref, g_ref, planes_ref, columns_ref, held, tile_sems, column_sems):
    cx, cy, cz = p_ref.shape
    step = LANES // cy
    half = cx // 2
    fetches = []
    for part in range(2):
        for which, ref in enumerate((p_ref, d_ref, g_ref)):
            at = pl.ds(part * half, half)
            fetches.append(
                pltpu.make_async_copy(
                    ref.at[at, :, pl.ds(cz - LANES, LANES)], held.at[which, at], tile_sems.at[part, which]
                )
            )
    for side, (outer, inner) in enumerate(((0, 1), (cy - 1, cy - 2))):
        for k, (ref, y) in enumerate(((p_ref, outer), (p_ref, inner), (d_ref, outer), (g_ref, outer))):
            at = 4 * side + k
            fetches.append(pltpu.make_async_copy(ref.at[:, y, :], columns_ref.at[at], column_sems.at[at]))
    for fetch in fetches:
        fetch.start()
    planes_ref[7:8] = jnp.zeros((1, cx * cy), F32)
    for part in range(2):
        for fetch in fetches[3 * part : 3 * part + 3]:
            fetch.wait()
        for k in range(part * half // step, (part + 1) * half // step):
            lanes = slice(k * LANES, (k + 1) * LANES)
            turned = [held[which, k * step : (k + 1) * step].reshape(LANES, LANES).T for which in range(3)]
            for row, (which, back) in enumerate(((0, 1), (0, 2), (0, 3), (1, 1), (1, 2), (2, 1), (2, 2))):
                line = turned[which][LANES - back : LANES - back + 1]
                planes_ref[row : row + 1, lanes] = 1.0 / (6.0 + line) if which == 2 else line
    for fetch in fetches[6:]:
        fetch.wait()


def slab(p, d, g):
    cx, cy, cz = p.shape
    return pl.pallas_call(
        slab_kernel,
        out_shape=(pltpu.VMEM((8, cx * cy), F32), pltpu.VMEM((8, cx, cz), F32)),
        in_specs=[ANY] * 3,
        out_specs=(VMEM, VMEM),
        scratch_shapes=[
            pltpu.VMEM((3, cx, cy, LANES), F32),
            pltpu.SemaphoreType.DMA((2, 3)),
            pltpu.SemaphoreType.DMA((8,)),
        ],
        compiler_params=limit(8),
        name="slab",
    )(in_hbm(p), in_hbm(d), in_hbm(g))


def in_hbm(array):
    return pltpu.with_memory_space_constraint(array, pltpu.HBM)


def in_vmem(array):
    return pltpu.with_memory_space_constraint(array, pltpu.VMEM)


def limit(mib):
    return pltpu.CompilerParams(vmem_limit_bytes=mib * 1024 * 1024)


def rolled(block, shift, axis=1):
    return pltpu.roll(block, shift % block.shape[axis], axis)


def packed(parts, cy):
    place = lax.rem(iota(parts[0].shape, 1) + 2, cy) // 4
    out = parts[0]
    for k in range(1, 4):
        out = jnp.where(place == k, rolled(parts[k], 4 * k), out)
    return out


def surface_kernel(cy, even_ref, planes_ref, first_ref, second_ref, normals_ref, traction_ref, gram_ref, out_ref, scratch):
    rows = planes_ref.shape[1]
    tiles = rows // LANES
    first, second = first_ref[:, first_ref.shape[1] - LANES :], second_ref[:, first_ref.shape[1] - LANES :]
    even = even_ref[0] == 1
    lane = iota((8, LANES), 1)

    def tile(face, above):
        turned = jnp.concatenate([face, jnp.zeros((LANES - face.shape[0], LANES), F32)], axis=0).T[LANES - 8 :]
        nearest = turned if above else rolled(turned, -cy)
        at = lambda k, back: rolled(nearest, -k * cy)[8 - back : 9 - back]
        blank = jnp.zeros((1, LANES), F32)
        next_out = turned[7:8] if above else rolled(turned, -3 * cy)[7:8]
        near = lane[:1] < cy if above else lane[:1] >= LANES - cy
        return jnp.concatenate(
            [jnp.where(near, at(0, 1), next_out), at(0, 2), blank, at(2, 1), blank, at(3, 1), blank, blank], axis=0
        )

    below, above = tile(jnp.where(even, second, first), False), tile(jnp.where(even, first, second), True)
    ext = jnp.concatenate([below, planes_ref[...], above], axis=1)
    y = lax.rem(iota(ext.shape, 1), cy)

    def around(block):
        inner = jnp.where(y == 0, 0.0, rolled(block, 1)) + jnp.where(y == cy - 1, 0.0, rolled(block, -1))
        return rolled(block, cy) + rolled(block, -cy) + inner

    def line(row):
        return ext[row : row + 1]

    near = around(ext)
    once = (line(3) + near[0:1] + line(1)) * line(5)
    beneath = (line(4) + near[1:2] + line(0) + line(2)) * line(6)
    twice = (line(3) + around(jnp.broadcast_to(once, ext.shape))[0:1] + beneath) * line(5)
    surface = twice[:, LANES : LANES + rows]
    normals = normals_ref[...]
    forces = normals * surface + traction_ref[...]
    own = slice(LANES, LANES + rows)
    wide = lambda part: jnp.broadcast_to(part, (8, rows))
    first = packed(
        [wide(normals[0:1]), wide(normals[1:2]), wide(normals[2:3]), wide(line(0)[:, own])], cy
    )
    second = packed(
        [wide(part[:, own]) for part in (line(1), once, line(5), line(5) * line(6))], cy
    )
    for t in range(tiles):
        lanes = slice(t * LANES, (t + 1) * LANES)
        for c in range(3):
            scratch[c * tiles + t : c * tiles + t + 1] = forces[c : c + 1, lanes]
        scratch[3 * tiles + t : 3 * tiles + t + 1] = first[0:1, lanes]
        scratch[4 * tiles + t : 4 * tiles + t + 1] = second[0:1, lanes]
    low, high = below, above
    side = jnp.where(
        lane < cy,
        rolled(low, cy)[0:1],
        jnp.where(
            lane < 2 * cy,
            rolled(high, cy)[0:1],
            jnp.where(lane < 3 * cy, rolled(low, 3 * cy)[5:6], rolled(high, 3 * cy)[5:6]),
        ),
    )
    scratch[5 * tiles : 5 * tiles + 8] = side
    scratch[5 * tiles + 8 :] = gram_ref[...]
    for d in range(out_ref.shape[0]):
        out_ref[d] = scratch[...]


def surface_message(count, cy, even, planes, first, second, normals, traction, gram):
    rows = 5 * planes.shape[1] // LANES + 8 + gram.shape[0]
    return pl.pallas_call(
        functools.partial(surface_kernel, cy),
        out_shape=jax.ShapeDtypeStruct((count, rows, LANES), F32),
        in_specs=[SMEM] + [VMEM] * 6,
        out_specs=VMEM,
        scratch_shapes=[pltpu.VMEM((rows, LANES), F32)],
        compiler_params=limit(8),
        name="surface",
    )(even, in_vmem(planes), first, second, normals, traction, gram)


def corrected(cy, got_ref, tiles, forces_ref):
    sources = got_ref.shape[0]
    rows = tiles * LANES

    def plane(index):
        return jnp.concatenate([got_ref[:, index * tiles + t, :] for t in range(tiles)], axis=1)

    def across(block):
        y, source = lax.rem(iota(block.shape, 1), cy), iota(block.shape, 0)
        before = rolled(rolled(block, 1, 0), 1 - cy)
        after = rolled(rolled(block, -1, 0), cy - 1)
        return jnp.where(
            (y == 0) & (source > 0), before, jnp.where((y == cy - 1) & (source < sources - 1), after, 0.0)
        )

    first, second = plane(3), plane(4)
    y = lax.rem(iota(first.shape, 1), cy)
    lane = iota(first.shape, 1)
    edge = lax.rem(y + 2, cy) < 4
    ratio = jnp.where(edge, rolled(second, -8), 0.0)
    both = jnp.where(edge, rolled(second, -12), 0.0)
    delta = ratio * across(rolled(first, -12))
    side = got_ref[:, 5 * tiles, :]
    side = rolled(side, -2 * cy) * across(side)
    end = jnp.concatenate([side] + [jnp.zeros_like(side)] * (tiles - 2) + [rolled(side, -2 * cy)], axis=1)
    total = jnp.where(lane < cy, end, rolled(delta, cy)) + jnp.where(lane >= rows - cy, end, rolled(delta, -cy))
    total += across(rolled(second, -4) + delta)
    total += jnp.where(y == 1, rolled(delta, 1), 0.0) + jnp.where(y == cy - 2, rolled(delta, -1), 0.0)
    change = ratio * total + both * across(second)
    for c in range(3):
        normal = jnp.where(edge, rolled(first, -4 * c), 0.0)
        forces = plane(c) + normal * change
        for t in range(tiles):
            forces_ref[c * tiles + t] = forces[:, t * LANES : (t + 1) * LANES]


def place_kernel(cy, place_ref, count_ref, got_ref, slot_ref, previous_ref, v_ref, owned_ref, message_ref, gram_scratch, forces_ref, held_v, arrived):
    own = place_ref[0]
    sources, tiles = got_ref.shape[0], slot_ref.shape[0] // got_ref.shape[0]
    capacity = previous_ref.shape[1]
    high = capacity // LANES
    base = own * capacity
    fetch = pltpu.make_async_copy(v_ref, held_v, arrived)
    fetch.start()
    corrected(cy, got_ref, tiles, forces_ref)

    def one_source(source, total):
        left, right = [], []
        for t in range(tiles):
            slots = slot_ref[pl.ds(source * tiles + t, 1), :]
            at_row = lax.shift_right_arithmetic(slots - base, 7) == iota((high, LANES), 0)
            right.append((jnp.bitwise_and(slots, LANES - 1) == iota((LANES, LANES), 0)).astype(F32))
            rough, fine = [], []
            for c in range(3):
                value = forces_ref[c * tiles + t, pl.ds(source, 1), :]
                near = value.astype(BF16).astype(F32)
                rough.append(jnp.where(at_row, near, 0.0))
                fine.append(jnp.where(at_row, value - near, 0.0))
            left.append(jnp.concatenate(rough + fine, axis=0))
        left = jnp.concatenate(left, axis=1).astype(BF16)
        right = jnp.concatenate(right, axis=1).astype(BF16)
        return total + lax.dot_general(
            left, right, (((1,), (1,)), ((), ())), preferred_element_type=F32
        )

    total = lax.fori_loop(0, sources, one_source, jnp.zeros((6 * high, LANES), F32), unroll=8)
    owned = total[: 3 * high] + total[3 * high :]
    fetch.wait()
    summed = jnp.zeros((v_ref.shape[1], LANES), F32)
    for c in range(3):
        for h in range(high):
            lanes = slice(h * LANES, (h + 1) * LANES)
            row = owned[c * high + h : c * high + h + 1]
            owned_ref[c : c + 1, lanes] = row
            held = iota((1, LANES), 1) + h * LANES < count_ref[0]
            residual = jnp.where(held, row - previous_ref[c : c + 1, lanes], 0.0)
            summed += held_v[c, :, lanes] * residual
    projection = lax.dot_general(
        jnp.ones((8, LANES), F32), summed, (((1,), (1,)), ((), ())), precision=HIGHEST, preferred_element_type=F32
    )
    gram_rows = gram_scratch.shape[0]
    gram_scratch[...] = jnp.sum(got_ref[:, 5 * tiles + 8 :, :], axis=0)
    chunk = gram_scratch[pl.ds(jnp.minimum(own, gram_rows - 1), 1), :]
    message = jnp.concatenate(
        [
            jnp.where(own < gram_rows, chunk, 0.0),
            projection[:1],
            jnp.zeros((1, LANES - projection.shape[1]), F32),
        ],
        axis=1,
    )
    message_ref[...] = jnp.broadcast_to(message[None], message_ref.shape)


def place(devices, cy, own, counts, got, slots, previous, v):
    columns = v.shape[1]
    return pl.pallas_call(
        functools.partial(place_kernel, cy),
        out_shape=(
            jax.ShapeDtypeStruct(previous.shape, F32),
            jax.ShapeDtypeStruct((devices, 1, 2 * LANES), F32),
        ),
        in_specs=[SMEM, SMEM, VMEM, VMEM, VMEM, ANY],
        out_specs=(VMEM, VMEM),
        scratch_shapes=[
            pltpu.VMEM((columns * columns // LANES, LANES), F32),
            pltpu.VMEM((3 * slots.shape[0] // got.shape[0], got.shape[0], LANES), F32),
            pltpu.VMEM(v.shape, F32),
            pltpu.SemaphoreType.DMA,
        ],
        compiler_params=limit(12),
        name="place",
    )(own, counts, got, slots, previous, v)


def solve_kernel(groups, count_ref, got_ref, owned_ref, w_ref, coupled_ref, held_w, arrived):
    fetch = pltpu.make_async_copy(w_ref, held_w, arrived)
    fetch.start()
    columns, capacity = w_ref.shape[1], w_ref.shape[2]
    gram_rows = columns * columns // LANES
    per_group = got_ref.shape[0] // groups
    tile = got_ref[:gram_rows, 0, :LANES]
    for g in range(1, groups):
        tile += got_ref[g * per_group : g * per_group + gram_rows, 0, :LANES]
    projection = jnp.sum(got_ref[:, 0, LANES:], axis=0, keepdims=True)
    gram = jnp.concatenate([tile[:, j : j + columns] for j in range(0, LANES, columns)], axis=0)
    rows, lanes = iota((columns, LANES), 0), iota((columns, LANES), 1)
    right = jnp.sum(jnp.where(rows == lanes, projection, 0.0), axis=1, keepdims=True)
    system = jnp.concatenate([gram, jnp.zeros((columns, LANES - columns), F32)], axis=1)
    system = jnp.where(lanes == columns, right, system)
    block = 8
    for k in range(0, columns, block):
        pivots = [system[k + i : k + i + 1] for i in range(block)]
        entry = [
            [jnp.broadcast_to(pivots[i][:, k + j : k + j + 1], (1, LANES)) for j in range(block)]
            for i in range(block)
        ]
        for i in range(block):
            inverse = 1.0 / entry[i][i]
            pivots[i] = pivots[i] * inverse
            entry[i] = [part * inverse if j > i else part for j, part in enumerate(entry[i])]
            for m in range(block):
                if m != i:
                    share = entry[m][i]
                    pivots[m] = pivots[m] - share * pivots[i]
                    entry[m] = [
                        part - share * entry[i][j] if j > i else part for j, part in enumerate(entry[m])
                    ]
        rest = system
        for i in range(block):
            rest = rest - system[:, k + i : k + i + 1] * pivots[i]
        for i in range(block):
            rest = jnp.where(rows == k + i, pivots[i], rest)
        system = rest
    coefficient = -system[:, columns : columns + 1]
    fetch.wait()
    for c in range(3):
        for h in range(capacity // LANES):
            at = slice(h * LANES, (h + 1) * LANES)
            update = jnp.sum(held_w[c, :, at] * coefficient, axis=0, keepdims=True)
            held = iota((1, LANES), 1) + h * LANES < count_ref[0]
            coupled_ref[c : c + 1, at] = jnp.where(held, owned_ref[c : c + 1, at] + update, 0.0)


def solve(groups, counts, got, owned, w):
    return pl.pallas_call(
        functools.partial(solve_kernel, groups),
        out_shape=jax.ShapeDtypeStruct(owned.shape, F32),
        in_specs=[SMEM, VMEM, VMEM, ANY],
        out_specs=VMEM,
        scratch_shapes=[pltpu.VMEM(w.shape, F32), pltpu.SemaphoreType.DMA],
        compiler_params=limit(8),
        name="solve",
    )(counts, got, owned, w)


def shifted(here, low, high):
    y, z = iota(here.shape, 0), iota(here.shape, 1)
    before = jnp.where(y == 0, low, rolled(here, 1, 0))
    after = jnp.where(y == here.shape[0] - 1, high, rolled(here, -1, 0))
    left = jnp.where(z == 0, 0.0, rolled(here, 1))
    right = jnp.where(z == here.shape[1] - 1, 0.0, rolled(here, -1))
    return before + after + left + right


CHUNK = 8


def halo_plane(even, first_ref, second_ref, k, above, cy):
    rows = slice(k * cy, (k + 1) * cy)
    return jnp.where(even != above, second_ref[rows], first_ref[rows])


def edge_kernel(
    cy, even_x_ref, even_y_ref, held, first_ref, second_ref, y_first_ref, y_second_ref, to_first_ref, to_second_ref
):
    cx, cz = held.shape[1:]
    even_x, even_y = even_x_ref[0] == 1, even_y_ref[0] == 1
    x, z = iota((cx, cz), 0), iota((cx, cz), 1)
    rows = []
    for side, y in enumerate((0, cy - 1)):
        here, inner, source, diagonal = [held[4 * side + k] for k in range(4)]
        below = halo_plane(even_x, first_ref, second_ref, 0, False, cy)[y : y + 1]
        above = halo_plane(even_x, first_ref, second_ref, 0, True, cy)[y : y + 1]
        total = source + inner + jnp.where(even_y != (side == 1), y_second_ref[...], y_first_ref[...])
        total += jnp.where(x == 0, below, rolled(here, 1, 0)) + jnp.where(x == cx - 1, above, rolled(here, -1, 0))
        total += jnp.where(z == 0, 0.0, rolled(here, 1)) + jnp.where(z == cz - 1, 0.0, rolled(here, -1))
        once = total * (1.0 / (6.0 + diagonal))
        rows.append((once, jnp.concatenate([below, above, jnp.zeros((6, cz), F32)], axis=0)))
    for at, k in ((slice(0, cx), 0), (slice(cx, cx + 8), 1)):
        to_first_ref[at] = jnp.where(even_y, rows[1][k], rows[0][k])
        to_second_ref[at] = jnp.where(even_y, rows[0][k], rows[1][k])


def swept_edges(even_x, even_y, cy, columns, first, second, y_first, y_second):
    cx, cz = columns.shape[1:]
    out = jax.ShapeDtypeStruct((cx + 8, cz), F32)
    return pl.pallas_call(
        functools.partial(edge_kernel, cy),
        out_shape=(out, out),
        in_specs=[SMEM, SMEM] + [VMEM] * 5,
        out_specs=(VMEM, VMEM),
        compiler_params=limit(8),
        name="edges",
    )(even_x, even_y, in_vmem(columns), first, second, y_first, y_second)


def sweeps_kernel(
    even_x_ref, even_y_ref, p_ref, d_ref, g_ref, first_ref, second_ref, y_first_ref, y_second_ref,
    far_first_ref, far_second_ref, out_ref, held_p, held_d, held_g, once_ref, rows_ref, in_sems, out_sems,
):
    cx, cy, cz = p_ref.shape
    steps = cx // CHUNK
    even_x, even_y = even_x_ref[0] == 1, even_y_ref[0] == 1

    def arrive(at):
        planes = pl.ds(at * CHUNK, CHUNK)
        return [
            pltpu.make_async_copy(ref.at[planes], held.at[planes], in_sems.at[k, at])
            for k, (ref, held) in enumerate(((p_ref, held_p), (d_ref, held_d), (g_ref, held_g)))
        ]

    def leave(at):
        planes = pl.ds(at * CHUNK, CHUNK)
        return pltpu.make_async_copy(held_p.at[planes], out_ref.at[planes], out_sems.at[at])

    for at in range(steps):
        for copy in arrive(at):
            copy.start()
    for k, (one, two) in enumerate(((y_first_ref, y_second_ref), (far_first_ref, far_second_ref))):
        rows_ref[2 * k, : one.shape[0]] = jnp.where(even_y, two[...], one[...])
        rows_ref[2 * k + 1, : one.shape[0]] = jnp.where(even_y, one[...], two[...])
    halo = lambda k, above: halo_plane(even_x, first_ref, second_ref, k, above, cy)

    def sweep(before, here, after, source, ratio, low, high):
        return (source + before + after + shifted(here, low, high)) * ratio

    def rows(k, at):
        return [rows_ref[2 * k + side, pl.ds(pl.multiple_of(at * CHUNK, CHUNK), CHUNK), :] for side in range(2)]

    for copy in arrive(0):
        copy.wait()

    def first_chunk(at, carry):
        @pl.when(at + 1 < steps)
        def _():
            for copy in arrive(jnp.minimum(at + 1, steps - 1)):
                copy.wait()

        before, here = carry
        lows, highs = rows(0, at)
        for j in range(CHUNK):
            x = at * CHUNK + j
            after = held_p[jnp.minimum(x + 1, cx - 1)]
            if j == CHUNK - 1:
                after = jnp.where(x == cx - 1, halo(0, True), after)
            ratio = 1.0 / (6.0 + held_g[x])
            once_ref[x] = sweep(before, here, after, held_d[x], ratio, lows[j : j + 1], highs[j : j + 1])
            held_g[x] = ratio
            before, here = here, after
        return before, here

    lax.fori_loop(0, steps, first_chunk, (halo(0, False), held_p[0]))
    ends = [rows_ref[2 + side, cx : cx + 8] for side in range(2)]
    start = sweep(
        halo(1, False), halo(0, False), held_p[0], halo(2, False), halo(3, False), ends[0][:1], ends[1][:1]
    )
    once_ref[cx] = sweep(
        held_p[cx - 1], halo(0, True), halo(1, True), halo(2, True), halo(3, True), ends[0][1:2], ends[1][1:2]
    )

    def second_chunk(at, carry):
        before, here = carry
        lows, highs = rows(1, at)
        for j in range(CHUNK):
            x = at * CHUNK + j
            after = once_ref[x + 1]
            held_p[x] = sweep(before, here, after, held_d[x], held_g[x], lows[j : j + 1], highs[j : j + 1])
            before, here = here, after
        leave(at).start()
        return before, here

    lax.fori_loop(0, steps, second_chunk, (start, once_ref[0]))
    for at in range(steps):
        leave(at).wait()


def both_sweeps(even_x, even_y, p, d, g, *beside):
    cx, cy, cz = p.shape
    return pl.pallas_call(
        sweeps_kernel,
        out_shape=jax.ShapeDtypeStruct(p.shape, F32),
        in_specs=[SMEM, SMEM] + [ANY] * 3 + [VMEM] * 6,
        out_specs=ANY,
        scratch_shapes=[pltpu.VMEM(p.shape, F32)] * 3
        + [
            pltpu.VMEM((cx + 1, cy, cz), F32),
            pltpu.VMEM((4, cx + 8, cz), F32),
            pltpu.SemaphoreType.DMA((3, cx // CHUNK)),
            pltpu.SemaphoreType.DMA((cx // CHUNK,)),
        ],
        compiler_params=limit(20),
        name="sweeps",
    )(even_x, even_y, in_hbm(p), in_hbm(d), in_hbm(g), *beside)


def shards(
    pressure, divergence, diagonal, normals, traction, slot_of, counts, previous, secant_v, secant_w
):
    groups, owners = lax.axis_size("gx"), lax.axis_size("gy")
    cy = pressure.shape[1]
    v = jnp.transpose(secant_v, (1, 0, 2))
    w = jnp.transpose(secant_w, (1, 0, 2))
    own = lax.axis_index("gy").astype(jnp.int32).reshape(1)
    even_x, even_y = [(1 - lax.axis_index(axis) % 2).astype(jnp.int32).reshape(1) for axis in ("gx", "gy")]
    fluid = (even_x, even_y, pressure, divergence, diagonal)
    first, second, y_first, y_second = outer_faces(*fluid)
    faces = traded(first, second, "gx")
    y_edges = traded(y_first, y_second, "gy")
    planes, columns = slab(pressure, divergence, diagonal)
    faces, y_edges = lax.optimization_barrier((faces, y_edges))
    gram = gram_tile(counts, v)
    block = surface_message(owners, cy, even_x, planes, *faces, normals, traction, gram)
    got = lax.all_to_all(block, "gy", 0, 0, tiled=True)
    far_edges = traded(*swept_edges(even_x, even_y, cy, columns, *faces, *y_edges), "gy")
    owned, message = place(
        groups * owners, cy, own, counts, got, slot_of.reshape(-1, LANES), previous, v
    )
    shared = lax.all_to_all(message, ("gx", "gy"), 0, 0, tiled=True)
    field = both_sweeps(*fluid, *faces, *y_edges, *far_edges)
    coupled = solve(groups, counts, shared, owned, w)
    return (field, coupled)


def solution(mesh):
    placed = (
        P("gx", "gy", None),
        P("gx", "gy", None),
        P("gx", "gy", None),
        P(None, ("gx", "gy")),
        P(None, ("gx", "gy")),
        P("gx", None),
        P(("gx", "gy")),
        P(None, ("gx", "gy")),
        P(None, None, ("gx", "gy")),
        P(None, None, ("gx", "gy")),
    )
    return jax.shard_map(
        shards,
        mesh=mesh,
        in_specs=placed,
        out_specs=(P("gx", "gy", None), P(None, ("gx", "gy"))),
        check_vma=False,
    )
```

```python
import functools
import jax
import jax.numpy as jnp
from jax import lax
from jax.experimental import pallas as pl
from jax.experimental.pallas import tpu as pltpu
from jax.sharding import PartitionSpec as P

LANES = 128
F32 = jnp.float32
BF16 = jnp.bfloat16
VMEM = pl.BlockSpec(memory_space=pltpu.VMEM)
ANY = pl.BlockSpec(memory_space=pl.ANY)
SMEM = pl.BlockSpec(memory_space=pltpu.SMEM)
HIGHEST = lax.Precision.HIGHEST


def pairs(count, parity):
    out = []
    for low in range(parity, count - 1, 2):
        out += [(low, low + 1), (low + 1, low)]
    return out


def traded(first, second, axis):
    count = lax.axis_size(axis)
    return lax.ppermute(first, axis, pairs(count, 0)), lax.ppermute(second, axis, pairs(count, 1))


def iota(shape, dim):
    return lax.broadcasted_iota(jnp.int32, shape, dim)


def occupied_rows(count, capacity):
    return (iota((1, capacity), 1) < count).astype(F32)


def gram_kernel(count_ref, v_ref, gram_ref):
    columns, capacity = v_ref.shape[1], v_ref.shape[2]
    occupied = occupied_rows(count_ref[0], capacity)
    total = jnp.zeros((columns, columns), F32)
    for c in range(v_ref.shape[0]):
        plain = v_ref[c]
        total += lax.dot_general(
            plain * occupied, plain, (((1,), (1,)), ((), ())), precision=HIGHEST, preferred_element_type=F32
        )
    rows = gram_ref.shape[0]
    gram_ref[...] = jnp.concatenate([total[j : j + rows] for j in range(0, columns, rows)], axis=1)


def gram_tile(counts, v):
    columns = v.shape[1]
    return pl.pallas_call(
        gram_kernel,
        out_shape=jax.ShapeDtypeStruct((columns * columns // LANES, LANES), F32),
        in_specs=[SMEM, VMEM],
        out_specs=VMEM,
        compiler_params=limit(8),
        name="gram",
    )(counts, v)


def faces_kernel(
    even_x_ref, even_y_ref, p_ref, d_ref, g_ref, first_ref, second_ref, y_first_ref, y_second_ref,
    ratios, face_sems, y_sems,
):
    cx, cy, cz = p_ref.shape
    even_x, even_y = even_x_ref[0] == 1, even_y_ref[0] == 1

    def face(out_ref, side, sources):
        return [
            pltpu.make_async_copy(
                ref.at[plane],
                ratios.at[side] if k == 3 else out_ref.at[pl.ds(k * cy, cy)],
                face_sems.at[side, k],
            )
            for k, (ref, plane) in enumerate(sources)
        ]

    def edge(out_ref, y, at):
        return pltpu.make_async_copy(p_ref.at[:, y, :], out_ref, y_sems.at[at])

    head = ((p_ref, 0), (p_ref, 1), (d_ref, 0), (g_ref, 0))
    tail = ((p_ref, cx - 1), (p_ref, cx - 2), (d_ref, cx - 1), (g_ref, cx - 1))

    @pl.when(even_x)
    def _():
        for copy in face(second_ref, 0, head) + face(first_ref, 1, tail):
            copy.start()

    @pl.when(~even_x)
    def _():
        for copy in face(first_ref, 0, head) + face(second_ref, 1, tail):
            copy.start()

    @pl.when(even_y)
    def _():
        edge(y_first_ref, cy - 1, 0).start()
        edge(y_second_ref, 0, 1).start()

    @pl.when(~even_y)
    def _():
        edge(y_first_ref, 0, 0).start()
        edge(y_second_ref, cy - 1, 1).start()

    for copy in face(first_ref, 0, head) + face(first_ref, 1, tail):
        copy.wait()
    low, high = 1.0 / (6.0 + ratios[0]), 1.0 / (6.0 + ratios[1])
    for out_ref, above in ((first_ref, even_x), (second_ref, ~even_x)):
        out_ref[3 * cy :] = jnp.where(above, high, low)
    edge(y_first_ref, 0, 0).wait()
    edge(y_second_ref, 0, 1).wait()


def outer_faces(even_x, even_y, p, d, g):
    cx, cy, cz = p.shape
    face = jax.ShapeDtypeStruct((4 * cy, cz), F32)
    edge = jax.ShapeDtypeStruct((cx, cz), F32)
    return pl.pallas_call(
        faces_kernel,
        out_shape=(face, face, edge, edge),
        in_specs=[SMEM, SMEM] + [ANY] * 3,
        out_specs=(VMEM,) * 4,
        scratch_shapes=[
            pltpu.VMEM((2, cy, cz), F32),
            pltpu.SemaphoreType.DMA((2, 4)),
            pltpu.SemaphoreType.DMA((2,)),
        ],
        compiler_params=limit(8),
        name="faces",
    )(even_x, even_y, in_hbm(p), in_hbm(d), in_hbm(g))


def slab_kernel(p_ref, d_ref, g_ref, planes_ref, columns_ref, held, tile_sems, column_sems):
    cx, cy, cz = p_ref.shape
    step = LANES // cy
    half = cx // 2
    fetches = []
    for part in range(2):
        for which, ref in enumerate((p_ref, d_ref, g_ref)):
            at = pl.ds(part * half, half)
            fetches.append(
                pltpu.make_async_copy(
                    ref.at[at, :, pl.ds(cz - LANES, LANES)], held.at[which, at], tile_sems.at[part, which]
                )
            )
    for side, (outer, inner) in enumerate(((0, 1), (cy - 1, cy - 2))):
        for k, (ref, y) in enumerate(((p_ref, outer), (p_ref, inner), (d_ref, outer), (g_ref, outer))):
            at = 4 * side + k
            fetches.append(pltpu.make_async_copy(ref.at[:, y, :], columns_ref.at[at], column_sems.at[at]))
    for fetch in fetches:
        fetch.start()
    planes_ref[7:8] = jnp.zeros((1, cx * cy), F32)
    for part in range(2):
        for fetch in fetches[3 * part : 3 * part + 3]:
            fetch.wait()
        for k in range(part * half // step, (part + 1) * half // step):
            lanes = slice(k * LANES, (k + 1) * LANES)
            turned = [held[which, k * step : (k + 1) * step].reshape(LANES, LANES).T for which in range(3)]
            for row, (which, back) in enumerate(((0, 1), (0, 2), (0, 3), (1, 1), (1, 2), (2, 1), (2, 2))):
                line = turned[which][LANES - back : LANES - back + 1]
                planes_ref[row : row + 1, lanes] = 1.0 / (6.0 + line) if which == 2 else line
    for fetch in fetches[6:]:
        fetch.wait()


def slab(p, d, g):
    cx, cy, cz = p.shape
    return pl.pallas_call(
        slab_kernel,
        out_shape=(pltpu.VMEM((8, cx * cy), F32), pltpu.VMEM((8, cx, cz), F32)),
        in_specs=[ANY] * 3,
        out_specs=(VMEM, VMEM),
        scratch_shapes=[
            pltpu.VMEM((3, cx, cy, LANES), F32),
            pltpu.SemaphoreType.DMA((2, 3)),
            pltpu.SemaphoreType.DMA((8,)),
        ],
        compiler_params=limit(8),
        name="slab",
    )(in_hbm(p), in_hbm(d), in_hbm(g))


def in_hbm(array):
    return pltpu.with_memory_space_constraint(array, pltpu.HBM)


def in_vmem(array):
    return pltpu.with_memory_space_constraint(array, pltpu.VMEM)


def limit(mib):
    return pltpu.CompilerParams(vmem_limit_bytes=mib * 1024 * 1024)


def rolled(block, shift, axis=1):
    return pltpu.roll(block, shift % block.shape[axis], axis)


def packed(parts, cy):
    place = lax.rem(iota(parts[0].shape, 1) + 2, cy) // 4
    out = parts[0]
    for k in range(1, 4):
        out = jnp.where(place == k, rolled(parts[k], 4 * k), out)
    return out


def surface_kernel(cy, even_ref, planes_ref, first_ref, second_ref, normals_ref, traction_ref, gram_ref, out_ref, scratch):
    rows = planes_ref.shape[1]
    tiles = rows // LANES
    first, second = first_ref[:, first_ref.shape[1] - LANES :], second_ref[:, first_ref.shape[1] - LANES :]
    even = even_ref[0] == 1
    lane = iota((8, LANES), 1)

    def tile(face, above):
        turned = jnp.concatenate([face, jnp.zeros((LANES - face.shape[0], LANES), F32)], axis=0).T[LANES - 8 :]
        nearest = turned if above else rolled(turned, -cy)
        at = lambda k, back: rolled(nearest, -k * cy)[8 - back : 9 - back]
        blank = jnp.zeros((1, LANES), F32)
        next_out = turned[7:8] if above else rolled(turned, -3 * cy)[7:8]
        near = lane[:1] < cy if above else lane[:1] >= LANES - cy
        return jnp.concatenate(
            [jnp.where(near, at(0, 1), next_out), at(0, 2), blank, at(2, 1), blank, at(3, 1), blank, blank], axis=0
        )

    below, above = tile(jnp.where(even, second, first), False), tile(jnp.where(even, first, second), True)
    ext = jnp.concatenate([below, planes_ref[...], above], axis=1)
    y = lax.rem(iota(ext.shape, 1), cy)

    def around(block):
        inner = jnp.where(y == 0, 0.0, rolled(block, 1)) + jnp.where(y == cy - 1, 0.0, rolled(block, -1))
        return rolled(block, cy) + rolled(block, -cy) + inner

    def line(row):
        return ext[row : row + 1]

    near = around(ext)
    once = (line(3) + near[0:1] + line(1)) * line(5)
    beneath = (line(4) + near[1:2] + line(0) + line(2)) * line(6)
    twice = (line(3) + around(jnp.broadcast_to(once, ext.shape))[0:1] + beneath) * line(5)
    surface = twice[:, LANES : LANES + rows]
    normals = normals_ref[...]
    forces = normals * surface + traction_ref[...]
    own = slice(LANES, LANES + rows)
    wide = lambda part: jnp.broadcast_to(part, (8, rows))
    first = packed(
        [wide(normals[0:1]), wide(normals[1:2]), wide(normals[2:3]), wide(line(0)[:, own])], cy
    )
    second = packed(
        [wide(part[:, own]) for part in (line(1), once, line(5), line(5) * line(6))], cy
    )
    for t in range(tiles):
        lanes = slice(t * LANES, (t + 1) * LANES)
        for c in range(3):
            scratch[c * tiles + t : c * tiles + t + 1] = forces[c : c + 1, lanes]
        scratch[3 * tiles + t : 3 * tiles + t + 1] = first[0:1, lanes]
        scratch[4 * tiles + t : 4 * tiles + t + 1] = second[0:1, lanes]
    low, high = below, above
    side = jnp.where(
        lane < cy,
        rolled(low, cy)[0:1],
        jnp.where(
            lane < 2 * cy,
            rolled(high, cy)[0:1],
            jnp.where(lane < 3 * cy, rolled(low, 3 * cy)[5:6], rolled(high, 3 * cy)[5:6]),
        ),
    )
    scratch[5 * tiles : 5 * tiles + 8] = side
    scratch[5 * tiles + 8 :] = gram_ref[...]
    for d in range(out_ref.shape[0]):
        out_ref[d] = scratch[...]


def surface_message(count, cy, even, planes, first, second, normals, traction, gram):
    rows = 5 * planes.shape[1] // LANES + 8 + gram.shape[0]
    return pl.pallas_call(
        functools.partial(surface_kernel, cy),
        out_shape=jax.ShapeDtypeStruct((count, rows, LANES), F32),
        in_specs=[SMEM] + [VMEM] * 6,
        out_specs=VMEM,
        scratch_shapes=[pltpu.VMEM((rows, LANES), F32)],
        compiler_params=limit(8),
        name="surface",
    )(even, in_vmem(planes), first, second, normals, traction, gram)


def corrected(cy, got_ref, tiles, forces_ref):
    sources = got_ref.shape[0]
    rows = tiles * LANES

    def plane(index):
        return jnp.concatenate([got_ref[:, index * tiles + t, :] for t in range(tiles)], axis=1)

    def across(block):
        y, source = lax.rem(iota(block.shape, 1), cy), iota(block.shape, 0)
        before = rolled(rolled(block, 1, 0), 1 - cy)
        after = rolled(rolled(block, -1, 0), cy - 1)
        return jnp.where(
            (y == 0) & (source > 0), before, jnp.where((y == cy - 1) & (source < sources - 1), after, 0.0)
        )

    first, second = plane(3), plane(4)
    y = lax.rem(iota(first.shape, 1), cy)
    lane = iota(first.shape, 1)
    edge = lax.rem(y + 2, cy) < 4
    ratio = jnp.where(edge, rolled(second, -8), 0.0)
    both = jnp.where(edge, rolled(second, -12), 0.0)
    delta = ratio * across(rolled(first, -12))
    side = got_ref[:, 5 * tiles, :]
    side = rolled(side, -2 * cy) * across(side)
    end = jnp.concatenate([side] + [jnp.zeros_like(side)] * (tiles - 2) + [rolled(side, -2 * cy)], axis=1)
    total = jnp.where(lane < cy, end, rolled(delta, cy)) + jnp.where(lane >= rows - cy, end, rolled(delta, -cy))
    total += across(rolled(second, -4) + delta)
    total += jnp.where(y == 1, rolled(delta, 1), 0.0) + jnp.where(y == cy - 2, rolled(delta, -1), 0.0)
    change = ratio * total + both * across(second)
    for c in range(3):
        normal = jnp.where(edge, rolled(first, -4 * c), 0.0)
        forces = plane(c) + normal * change
        for t in range(tiles):
            forces_ref[c * tiles + t] = forces[:, t * LANES : (t + 1) * LANES]


def place_kernel(cy, place_ref, count_ref, got_ref, slot_ref, previous_ref, v_ref, owned_ref, message_ref, gram_scratch, forces_ref, held_v, arrived):
    own = place_ref[0]
    sources, tiles = got_ref.shape[0], slot_ref.shape[0] // got_ref.shape[0]
    capacity = previous_ref.shape[1]
    high = capacity // LANES
    base = own * capacity
    fetch = pltpu.make_async_copy(v_ref, held_v, arrived)
    fetch.start()
    corrected(cy, got_ref, tiles, forces_ref)

    def one_source(source, total):
        left, right = [], []
        for t in range(tiles):
            slots = slot_ref[pl.ds(source * tiles + t, 1), :]
            at_row = lax.shift_right_arithmetic(slots - base, 7) == iota((high, LANES), 0)
            right.append((jnp.bitwise_and(slots, LANES - 1) == iota((LANES, LANES), 0)).astype(F32))
            rough, fine = [], []
            for c in range(3):
                value = forces_ref[c * tiles + t, pl.ds(source, 1), :]
                near = value.astype(BF16).astype(F32)
                rough.append(jnp.where(at_row, near, 0.0))
                fine.append(jnp.where(at_row, value - near, 0.0))
            left.append(jnp.concatenate(rough + fine, axis=0))
        left = jnp.concatenate(left, axis=1).astype(BF16)
        right = jnp.concatenate(right, axis=1).astype(BF16)
        return total + lax.dot_general(
            left, right, (((1,), (1,)), ((), ())), preferred_element_type=F32
        )

    total = lax.fori_loop(0, sources, one_source, jnp.zeros((6 * high, LANES), F32), unroll=8)
    owned = total[: 3 * high] + total[3 * high :]
    fetch.wait()
    summed = jnp.zeros((v_ref.shape[1], LANES), F32)
    for c in range(3):
        for h in range(high):
            lanes = slice(h * LANES, (h + 1) * LANES)
            row = owned[c * high + h : c * high + h + 1]
            owned_ref[c : c + 1, lanes] = row
            held = iota((1, LANES), 1) + h * LANES < count_ref[0]
            residual = jnp.where(held, row - previous_ref[c : c + 1, lanes], 0.0)
            summed += held_v[c, :, lanes] * residual
    projection = lax.dot_general(
        jnp.ones((8, LANES), F32), summed, (((1,), (1,)), ((), ())), precision=HIGHEST, preferred_element_type=F32
    )
    gram_rows = gram_scratch.shape[0]
    gram_scratch[...] = jnp.sum(got_ref[:, 5 * tiles + 8 :, :], axis=0)
    chunk = gram_scratch[pl.ds(jnp.minimum(own, gram_rows - 1), 1), :]
    message = jnp.concatenate(
        [
            jnp.where(own < gram_rows, chunk, 0.0),
            projection[:1],
            jnp.zeros((1, LANES - projection.shape[1]), F32),
        ],
        axis=1,
    )
    message_ref[...] = jnp.broadcast_to(message[None], message_ref.shape)


def place(devices, cy, own, counts, got, slots, previous, v):
    columns = v.shape[1]
    return pl.pallas_call(
        functools.partial(place_kernel, cy),
        out_shape=(
            jax.ShapeDtypeStruct(previous.shape, F32),
            jax.ShapeDtypeStruct((devices, 1, 2 * LANES), F32),
        ),
        in_specs=[SMEM, SMEM, VMEM, VMEM, VMEM, ANY],
        out_specs=(VMEM, VMEM),
        scratch_shapes=[
            pltpu.VMEM((columns * columns // LANES, LANES), F32),
            pltpu.VMEM((3 * slots.shape[0] // got.shape[0], got.shape[0], LANES), F32),
            pltpu.VMEM(v.shape, F32),
            pltpu.SemaphoreType.DMA,
        ],
        compiler_params=limit(12),
        name="place",
    )(own, counts, got, slots, previous, v)


def solve_kernel(groups, count_ref, got_ref, owned_ref, w_ref, coupled_ref, held_w, arrived):
    fetch = pltpu.make_async_copy(w_ref, held_w, arrived)
    fetch.start()
    columns, capacity = w_ref.shape[1], w_ref.shape[2]
    gram_rows = columns * columns // LANES
    per_group = got_ref.shape[0] // groups
    tile = got_ref[:gram_rows, 0, :LANES]
    for g in range(1, groups):
        tile += got_ref[g * per_group : g * per_group + gram_rows, 0, :LANES]
    projection = jnp.sum(got_ref[:, 0, LANES:], axis=0, keepdims=True)
    gram = jnp.concatenate([tile[:, j : j + columns] for j in range(0, LANES, columns)], axis=0)
    rows, lanes = iota((columns, LANES), 0), iota((columns, LANES), 1)
    right = jnp.sum(jnp.where(rows == lanes, projection, 0.0), axis=1, keepdims=True)
    system = jnp.concatenate([gram, jnp.zeros((columns, LANES - columns), F32)], axis=1)
    system = jnp.where(lanes == columns, right, system)
    block = 8
    for k in range(0, columns, block):
        pivots = [system[k + i : k + i + 1] for i in range(block)]
        entry = [
            [jnp.broadcast_to(pivots[i][:, k + j : k + j + 1], (1, LANES)) for j in range(block)]
            for i in range(block)
        ]
        for i in range(block):
            inverse = 1.0 / entry[i][i]
            pivots[i] = pivots[i] * inverse
            entry[i] = [part * inverse if j > i else part for j, part in enumerate(entry[i])]
            for m in range(block):
                if m != i:
                    share = entry[m][i]
                    pivots[m] = pivots[m] - share * pivots[i]
                    entry[m] = [
                        part - share * entry[i][j] if j > i else part for j, part in enumerate(entry[m])
                    ]
        rest = system
        for i in range(block):
            rest = rest - system[:, k + i : k + i + 1] * pivots[i]
        for i in range(block):
            rest = jnp.where(rows == k + i, pivots[i], rest)
        system = rest
    coefficient = -system[:, columns : columns + 1]
    fetch.wait()
    for c in range(3):
        for h in range(capacity // LANES):
            at = slice(h * LANES, (h + 1) * LANES)
            update = jnp.sum(held_w[c, :, at] * coefficient, axis=0, keepdims=True)
            held = iota((1, LANES), 1) + h * LANES < count_ref[0]
            coupled_ref[c : c + 1, at] = jnp.where(held, owned_ref[c : c + 1, at] + update, 0.0)


def solve(groups, counts, got, owned, w):
    return pl.pallas_call(
        functools.partial(solve_kernel, groups),
        out_shape=jax.ShapeDtypeStruct(owned.shape, F32),
        in_specs=[SMEM, VMEM, VMEM, ANY],
        out_specs=VMEM,
        scratch_shapes=[pltpu.VMEM(w.shape, F32), pltpu.SemaphoreType.DMA],
        compiler_params=limit(8),
        name="solve",
    )(counts, got, owned, w)


def shifted(here, low, high):
    y, z = iota(here.shape, 0), iota(here.shape, 1)
    before = jnp.where(y == 0, low, rolled(here, 1, 0))
    after = jnp.where(y == here.shape[0] - 1, high, rolled(here, -1, 0))
    left = jnp.where(z == 0, 0.0, rolled(here, 1))
    right = jnp.where(z == here.shape[1] - 1, 0.0, rolled(here, -1))
    return before + after + left + right


CHUNK = 8


def halo_plane(even, first_ref, second_ref, k, above, cy):
    rows = slice(k * cy, (k + 1) * cy)
    return jnp.where(even != above, second_ref[rows], first_ref[rows])


def edge_kernel(
    cy, even_x_ref, even_y_ref, held, first_ref, second_ref, y_first_ref, y_second_ref, to_first_ref, to_second_ref
):
    cx, cz = held.shape[1:]
    even_x, even_y = even_x_ref[0] == 1, even_y_ref[0] == 1
    x, z = iota((cx, cz), 0), iota((cx, cz), 1)
    rows = []
    for side, y in enumerate((0, cy - 1)):
        here, inner, source, diagonal = [held[4 * side + k] for k in range(4)]
        below = halo_plane(even_x, first_ref, second_ref, 0, False, cy)[y : y + 1]
        above = halo_plane(even_x, first_ref, second_ref, 0, True, cy)[y : y + 1]
        total = source + inner + jnp.where(even_y != (side == 1), y_second_ref[...], y_first_ref[...])
        total += jnp.where(x == 0, below, rolled(here, 1, 0)) + jnp.where(x == cx - 1, above, rolled(here, -1, 0))
        total += jnp.where(z == 0, 0.0, rolled(here, 1)) + jnp.where(z == cz - 1, 0.0, rolled(here, -1))
        once = total * (1.0 / (6.0 + diagonal))
        rows.append((once, jnp.concatenate([below, above, jnp.zeros((6, cz), F32)], axis=0)))
    for at, k in ((slice(0, cx), 0), (slice(cx, cx + 8), 1)):
        to_first_ref[at] = jnp.where(even_y, rows[1][k], rows[0][k])
        to_second_ref[at] = jnp.where(even_y, rows[0][k], rows[1][k])


def swept_edges(even_x, even_y, cy, columns, first, second, y_first, y_second):
    cx, cz = columns.shape[1:]
    out = jax.ShapeDtypeStruct((cx + 8, cz), F32)
    return pl.pallas_call(
        functools.partial(edge_kernel, cy),
        out_shape=(out, out),
        in_specs=[SMEM, SMEM] + [VMEM] * 5,
        out_specs=(VMEM, VMEM),
        compiler_params=limit(8),
        name="edges",
    )(even_x, even_y, in_vmem(columns), first, second, y_first, y_second)


def sweeps_kernel(
    even_x_ref, even_y_ref, p_ref, d_ref, g_ref, first_ref, second_ref, y_first_ref, y_second_ref,
    far_first_ref, far_second_ref, out_ref, held_p, held_d, held_g, once_ref, rows_ref, in_sems, out_sems,
):
    cx, cy, cz = p_ref.shape
    steps = cx // CHUNK
    even_x, even_y = even_x_ref[0] == 1, even_y_ref[0] == 1

    def arrive(at):
        planes = pl.ds(at * CHUNK, CHUNK)
        return [
            pltpu.make_async_copy(ref.at[planes], held.at[planes], in_sems.at[k, at])
            for k, (ref, held) in enumerate(((p_ref, held_p), (d_ref, held_d), (g_ref, held_g)))
        ]

    def leave(at):
        planes = pl.ds(at * CHUNK, CHUNK)
        return pltpu.make_async_copy(held_p.at[planes], out_ref.at[planes], out_sems.at[at])

    for at in range(steps):
        for copy in arrive(at):
            copy.start()
    for k, (one, two) in enumerate(((y_first_ref, y_second_ref), (far_first_ref, far_second_ref))):
        rows_ref[2 * k, : one.shape[0]] = jnp.where(even_y, two[...], one[...])
        rows_ref[2 * k + 1, : one.shape[0]] = jnp.where(even_y, one[...], two[...])
    halo = lambda k, above: halo_plane(even_x, first_ref, second_ref, k, above, cy)

    def sweep(before, here, after, source, ratio, low, high):
        return (source + before + after + shifted(here, low, high)) * ratio

    def rows(k, at):
        return [rows_ref[2 * k + side, pl.ds(pl.multiple_of(at * CHUNK, CHUNK), CHUNK), :] for side in range(2)]

    for copy in arrive(0):
        copy.wait()

    def first_chunk(at, carry):
        @pl.when(at + 1 < steps)
        def _():
            for copy in arrive(jnp.minimum(at + 1, steps - 1)):
                copy.wait()

        before, here = carry
        lows, highs = rows(0, at)
        for j in range(CHUNK):
            x = at * CHUNK + j
            after = held_p[jnp.minimum(x + 1, cx - 1)]
            if j == CHUNK - 1:
                after = jnp.where(x == cx - 1, halo(0, True), after)
            ratio = 1.0 / (6.0 + held_g[x])
            once_ref[x] = sweep(before, here, after, held_d[x], ratio, lows[j : j + 1], highs[j : j + 1])
            held_g[x] = ratio
            before, here = here, after
        return before, here

    lax.fori_loop(0, steps, first_chunk, (halo(0, False), held_p[0]))
    ends = [rows_ref[2 + side, cx : cx + 8] for side in range(2)]
    start = sweep(
        halo(1, False), halo(0, False), held_p[0], halo(2, False), halo(3, False), ends[0][:1], ends[1][:1]
    )
    once_ref[cx] = sweep(
        held_p[cx - 1], halo(0, True), halo(1, True), halo(2, True), halo(3, True), ends[0][1:2], ends[1][1:2]
    )

    def second_chunk(at, carry):
        before, here = carry
        lows, highs = rows(1, at)
        for j in range(CHUNK):
            x = at * CHUNK + j
            after = once_ref[x + 1]
            held_p[x] = sweep(before, here, after, held_d[x], held_g[x], lows[j : j + 1], highs[j : j + 1])
            before, here = here, after
        leave(at).start()
        return before, here

    lax.fori_loop(0, steps, second_chunk, (start, once_ref[0]))
    for at in range(steps):
        leave(at).wait()


def both_sweeps(even_x, even_y, p, d, g, *beside):
    cx, cy, cz = p.shape
    return pl.pallas_call(
        sweeps_kernel,
        out_shape=jax.ShapeDtypeStruct(p.shape, F32),
        in_specs=[SMEM, SMEM] + [ANY] * 3 + [VMEM] * 6,
        out_specs=ANY,
        scratch_shapes=[pltpu.VMEM(p.shape, F32)] * 3
        + [
            pltpu.VMEM((cx + 1, cy, cz), F32),
            pltpu.VMEM((4, cx + 8, cz), F32),
            pltpu.SemaphoreType.DMA((3, cx // CHUNK)),
            pltpu.SemaphoreType.DMA((cx // CHUNK,)),
        ],
        compiler_params=limit(20),
        name="sweeps",
    )(even_x, even_y, in_hbm(p), in_hbm(d), in_hbm(g), *beside)


def shards(
    pressure, divergence, diagonal, normals, traction, slot_of, counts, previous, secant_v, secant_w
):
    groups, owners = lax.axis_size("gx"), lax.axis_size("gy")
    cy = pressure.shape[1]
    v = jnp.transpose(secant_v, (1, 0, 2))
    w = jnp.transpose(secant_w, (1, 0, 2))
    own = lax.axis_index("gy").astype(jnp.int32).reshape(1)
    even_x, even_y = [(1 - lax.axis_index(axis) % 2).astype(jnp.int32).reshape(1) for axis in ("gx", "gy")]
    fluid = (even_x, even_y, pressure, divergence, diagonal)
    first, second, y_first, y_second = outer_faces(*fluid)
    y_edges = traded(y_first, y_second, "gy")
    faces = traded(first, second, "gx")
    planes, columns = slab(pressure, divergence, diagonal)
    y_edges, faces = lax.optimization_barrier((y_edges, faces))
    gram = gram_tile(counts, v)
    block = surface_message(owners, cy, even_x, planes, *faces, normals, traction, gram)
    got = lax.all_to_all(block, "gy", 0, 0, tiled=True)
    far_edges = traded(*swept_edges(even_x, even_y, cy, columns, *faces, *y_edges), "gy")
    owned, message = place(
        groups * owners, cy, own, counts, got, slot_of.reshape(-1, LANES), previous, v
    )
    shared = lax.all_to_all(message, ("gx", "gy"), 0, 0, tiled=True)
    field = both_sweeps(*fluid, *faces, *y_edges, *far_edges)
    coupled = solve(groups, counts, shared, owned, w)
    return (field, coupled)


def solution(mesh):
    placed = (
        P("gx", "gy", None),
        P("gx", "gy", None),
        P("gx", "gy", None),
        P(None, ("gx", "gy")),
        P(None, ("gx", "gy")),
        P("gx", None),
        P(("gx", "gy")),
        P(None, ("gx", "gy")),
        P(None, None, ("gx", "gy")),
        P(None, None, ("gx", "gy")),
    )
    return jax.shard_map(
        shards,
        mesh=mesh,
        in_specs=placed,
        out_specs=(P("gx", "gy", None), P(None, ("gx", "gy"))),
        check_vma=False,
    )
```

```python
import functools
import jax
import jax.numpy as jnp
from jax import lax
from jax.experimental import pallas as pl
from jax.experimental.pallas import tpu as pltpu
from jax.sharding import PartitionSpec as P

LANES = 128
F32 = jnp.float32
BF16 = jnp.bfloat16
VMEM = pl.BlockSpec(memory_space=pltpu.VMEM)
ANY = pl.BlockSpec(memory_space=pl.ANY)
SMEM = pl.BlockSpec(memory_space=pltpu.SMEM)
HIGHEST = lax.Precision.HIGHEST


def pairs(count, parity):
    out = []
    for low in range(parity, count - 1, 2):
        out += [(low, low + 1), (low + 1, low)]
    return out


def traded(first, second, axis):
    count = lax.axis_size(axis)
    return lax.ppermute(first, axis, pairs(count, 0)), lax.ppermute(second, axis, pairs(count, 1))


def iota(shape, dim):
    return lax.broadcasted_iota(jnp.int32, shape, dim)


def occupied_rows(count, capacity):
    return (iota((1, capacity), 1) < count).astype(F32)


def gram_kernel(count_ref, v_ref, gram_ref):
    columns, capacity = v_ref.shape[1], v_ref.shape[2]
    occupied = occupied_rows(count_ref[0], capacity)
    total = jnp.zeros((columns, columns), F32)
    for c in range(v_ref.shape[0]):
        plain = v_ref[c]
        total += lax.dot_general(
            plain * occupied, plain, (((1,), (1,)), ((), ())), precision=HIGHEST, preferred_element_type=F32
        )
    rows = gram_ref.shape[0]
    gram_ref[...] = jnp.concatenate([total[j : j + rows] for j in range(0, columns, rows)], axis=1)


def gram_tile(counts, v):
    columns = v.shape[1]
    return pl.pallas_call(
        gram_kernel,
        out_shape=jax.ShapeDtypeStruct((columns * columns // LANES, LANES), F32),
        in_specs=[SMEM, VMEM],
        out_specs=VMEM,
        compiler_params=limit(8),
        name="gram",
    )(counts, v)


def y_edges_kernel(even_ref, p_ref, first_ref, second_ref, sems):
    last = p_ref.shape[1] - 1

    def edge(out_ref, y, at):
        return pltpu.make_async_copy(p_ref.at[:, y, :], out_ref, sems.at[at])

    @pl.when(even_ref[0] == 1)
    def _():
        edge(first_ref, last, 0).start()
        edge(second_ref, 0, 1).start()

    @pl.when(even_ref[0] != 1)
    def _():
        edge(first_ref, 0, 0).start()
        edge(second_ref, last, 1).start()

    edge(first_ref, 0, 0).wait()
    edge(second_ref, 0, 1).wait()


def outer_y_edges(even_y, p):
    cx, cy, cz = p.shape
    edge = jax.ShapeDtypeStruct((cx, cz), F32)
    return pl.pallas_call(
        y_edges_kernel,
        out_shape=(edge, edge),
        in_specs=[SMEM, ANY],
        out_specs=(VMEM, VMEM),
        scratch_shapes=[pltpu.SemaphoreType.DMA((2,))],
        compiler_params=limit(8),
        name="y_edges",
    )(even_y, in_hbm(p))


def faces_kernel(
    even_x_ref, p_ref, d_ref, g_ref, first_ref, second_ref, ratios, face_sems
):
    cx, cy, cz = p_ref.shape
    even_x = even_x_ref[0] == 1

    def face(out_ref, side, sources):
        return [
            pltpu.make_async_copy(
                ref.at[plane],
                ratios.at[side] if k == 3 else out_ref.at[pl.ds(k * cy, cy)],
                face_sems.at[side, k],
            )
            for k, (ref, plane) in enumerate(sources)
        ]

    head = ((p_ref, 0), (p_ref, 1), (d_ref, 0), (g_ref, 0))
    tail = ((p_ref, cx - 1), (p_ref, cx - 2), (d_ref, cx - 1), (g_ref, cx - 1))

    @pl.when(even_x)
    def _():
        for copy in face(second_ref, 0, head) + face(first_ref, 1, tail):
            copy.start()

    @pl.when(~even_x)
    def _():
        for copy in face(first_ref, 0, head) + face(second_ref, 1, tail):
            copy.start()

    for copy in face(first_ref, 0, head) + face(first_ref, 1, tail):
        copy.wait()
    low, high = 1.0 / (6.0 + ratios[0]), 1.0 / (6.0 + ratios[1])
    for out_ref, above in ((first_ref, even_x), (second_ref, ~even_x)):
        out_ref[3 * cy :] = jnp.where(above, high, low)


def outer_faces(even_x, p, d, g):
    cx, cy, cz = p.shape
    face = jax.ShapeDtypeStruct((4 * cy, cz), F32)
    return pl.pallas_call(
        faces_kernel,
        out_shape=(face, face),
        in_specs=[SMEM] + [ANY] * 3,
        out_specs=(VMEM,) * 2,
        scratch_shapes=[
            pltpu.VMEM((2, cy, cz), F32),
            pltpu.SemaphoreType.DMA((2, 4)),
        ],
        compiler_params=limit(8),
        name="faces",
    )(even_x, in_hbm(p), in_hbm(d), in_hbm(g))


def slab_kernel(p_ref, d_ref, g_ref, planes_ref, columns_ref, held, tile_sems, column_sems):
    cx, cy, cz = p_ref.shape
    step = LANES // cy
    half = cx // 2
    fetches = []
    for part in range(2):
        for which, ref in enumerate((p_ref, d_ref, g_ref)):
            at = pl.ds(part * half, half)
            fetches.append(
                pltpu.make_async_copy(
                    ref.at[at, :, pl.ds(cz - LANES, LANES)], held.at[which, at], tile_sems.at[part, which]
                )
            )
    for side, (outer, inner) in enumerate(((0, 1), (cy - 1, cy - 2))):
        for k, (ref, y) in enumerate(((p_ref, outer), (p_ref, inner), (d_ref, outer), (g_ref, outer))):
            at = 4 * side + k
            fetches.append(pltpu.make_async_copy(ref.at[:, y, :], columns_ref.at[at], column_sems.at[at]))
    for fetch in fetches:
        fetch.start()
    planes_ref[7:8] = jnp.zeros((1, cx * cy), F32)
    for part in range(2):
        for fetch in fetches[3 * part : 3 * part + 3]:
            fetch.wait()
        for k in range(part * half // step, (part + 1) * half // step):
            lanes = slice(k * LANES, (k + 1) * LANES)
            turned = [held[which, k * step : (k + 1) * step].reshape(LANES, LANES).T for which in range(3)]
            for row, (which, back) in enumerate(((0, 1), (0, 2), (0, 3), (1, 1), (1, 2), (2, 1), (2, 2))):
                line = turned[which][LANES - back : LANES - back + 1]
                planes_ref[row : row + 1, lanes] = 1.0 / (6.0 + line) if which == 2 else line
    for fetch in fetches[6:]:
        fetch.wait()


def slab(p, d, g):
    cx, cy, cz = p.shape
    return pl.pallas_call(
        slab_kernel,
        out_shape=(pltpu.VMEM((8, cx * cy), F32), pltpu.VMEM((8, cx, cz), F32)),
        in_specs=[ANY] * 3,
        out_specs=(VMEM, VMEM),
        scratch_shapes=[
            pltpu.VMEM((3, cx, cy, LANES), F32),
            pltpu.SemaphoreType.DMA((2, 3)),
            pltpu.SemaphoreType.DMA((8,)),
        ],
        compiler_params=limit(8),
        name="slab",
    )(in_hbm(p), in_hbm(d), in_hbm(g))


def in_hbm(array):
    return pltpu.with_memory_space_constraint(array, pltpu.HBM)


def in_vmem(array):
    return pltpu.with_memory_space_constraint(array, pltpu.VMEM)


def limit(mib):
    return pltpu.CompilerParams(vmem_limit_bytes=mib * 1024 * 1024)


def rolled(block, shift, axis=1):
    return pltpu.roll(block, shift % block.shape[axis], axis)


def packed(parts, cy):
    place = lax.rem(iota(parts[0].shape, 1) + 2, cy) // 4
    out = parts[0]
    for k in range(1, 4):
        out = jnp.where(place == k, rolled(parts[k], 4 * k), out)
    return out


def surface_kernel(cy, even_ref, planes_ref, first_ref, second_ref, normals_ref, traction_ref, gram_ref, out_ref, scratch):
    rows = planes_ref.shape[1]
    tiles = rows // LANES
    first, second = first_ref[:, first_ref.shape[1] - LANES :], second_ref[:, first_ref.shape[1] - LANES :]
    even = even_ref[0] == 1
    lane = iota((8, LANES), 1)

    def tile(face, above):
        turned = jnp.concatenate([face, jnp.zeros((LANES - face.shape[0], LANES), F32)], axis=0).T[LANES - 8 :]
        nearest = turned if above else rolled(turned, -cy)
        at = lambda k, back: rolled(nearest, -k * cy)[8 - back : 9 - back]
        blank = jnp.zeros((1, LANES), F32)
        next_out = turned[7:8] if above else rolled(turned, -3 * cy)[7:8]
        near = lane[:1] < cy if above else lane[:1] >= LANES - cy
        return jnp.concatenate(
            [jnp.where(near, at(0, 1), next_out), at(0, 2), blank, at(2, 1), blank, at(3, 1), blank, blank], axis=0
        )

    below, above = tile(jnp.where(even, second, first), False), tile(jnp.where(even, first, second), True)
    ext = jnp.concatenate([below, planes_ref[...], above], axis=1)
    y = lax.rem(iota(ext.shape, 1), cy)

    def around(block):
        inner = jnp.where(y == 0, 0.0, rolled(block, 1)) + jnp.where(y == cy - 1, 0.0, rolled(block, -1))
        return rolled(block, cy) + rolled(block, -cy) + inner

    def line(row):
        return ext[row : row + 1]

    near = around(ext)
    once = (line(3) + near[0:1] + line(1)) * line(5)
    beneath = (line(4) + near[1:2] + line(0) + line(2)) * line(6)
    twice = (line(3) + around(jnp.broadcast_to(once, ext.shape))[0:1] + beneath) * line(5)
    surface = twice[:, LANES : LANES + rows]
    normals = normals_ref[...]
    forces = normals * surface + traction_ref[...]
    own = slice(LANES, LANES + rows)
    wide = lambda part: jnp.broadcast_to(part, (8, rows))
    first = packed(
        [wide(normals[0:1]), wide(normals[1:2]), wide(normals[2:3]), wide(line(0)[:, own])], cy
    )
    second = packed(
        [wide(part[:, own]) for part in (line(1), once, line(5), line(5) * line(6))], cy
    )
    for t in range(tiles):
        lanes = slice(t * LANES, (t + 1) * LANES)
        for c in range(3):
            scratch[c * tiles + t : c * tiles + t + 1] = forces[c : c + 1, lanes]
        scratch[3 * tiles + t : 3 * tiles + t + 1] = first[0:1, lanes]
        scratch[4 * tiles + t : 4 * tiles + t + 1] = second[0:1, lanes]
    low, high = below, above
    side = jnp.where(
        lane < cy,
        rolled(low, cy)[0:1],
        jnp.where(
            lane < 2 * cy,
            rolled(high, cy)[0:1],
            jnp.where(lane < 3 * cy, rolled(low, 3 * cy)[5:6], rolled(high, 3 * cy)[5:6]),
        ),
    )
    scratch[5 * tiles : 5 * tiles + 8] = side
    scratch[5 * tiles + 8 :] = gram_ref[...]
    for d in range(out_ref.shape[0]):
        out_ref[d] = scratch[...]


def surface_message(count, cy, even, planes, first, second, normals, traction, gram):
    rows = 5 * planes.shape[1] // LANES + 8 + gram.shape[0]
    return pl.pallas_call(
        functools.partial(surface_kernel, cy),
        out_shape=jax.ShapeDtypeStruct((count, rows, LANES), F32),
        in_specs=[SMEM] + [VMEM] * 6,
        out_specs=VMEM,
        scratch_shapes=[pltpu.VMEM((rows, LANES), F32)],
        compiler_params=limit(8),
        name="surface",
    )(even, in_vmem(planes), first, second, normals, traction, gram)


def corrected(cy, got_ref, tiles, forces_ref):
    sources = got_ref.shape[0]
    rows = tiles * LANES

    def plane(index):
        return jnp.concatenate([got_ref[:, index * tiles + t, :] for t in range(tiles)], axis=1)

    def across(block):
        y, source = lax.rem(iota(block.shape, 1), cy), iota(block.shape, 0)
        before = rolled(rolled(block, 1, 0), 1 - cy)
        after = rolled(rolled(block, -1, 0), cy - 1)
        return jnp.where(
            (y == 0) & (source > 0), before, jnp.where((y == cy - 1) & (source < sources - 1), after, 0.0)
        )

    first, second = plane(3), plane(4)
    y = lax.rem(iota(first.shape, 1), cy)
    lane = iota(first.shape, 1)
    edge = lax.rem(y + 2, cy) < 4
    ratio = jnp.where(edge, rolled(second, -8), 0.0)
    both = jnp.where(edge, rolled(second, -12), 0.0)
    delta = ratio * across(rolled(first, -12))
    side = got_ref[:, 5 * tiles, :]
    side = rolled(side, -2 * cy) * across(side)
    end = jnp.concatenate([side] + [jnp.zeros_like(side)] * (tiles - 2) + [rolled(side, -2 * cy)], axis=1)
    total = jnp.where(lane < cy, end, rolled(delta, cy)) + jnp.where(lane >= rows - cy, end, rolled(delta, -cy))
    total += across(rolled(second, -4) + delta)
    total += jnp.where(y == 1, rolled(delta, 1), 0.0) + jnp.where(y == cy - 2, rolled(delta, -1), 0.0)
    change = ratio * total + both * across(second)
    for c in range(3):
        normal = jnp.where(edge, rolled(first, -4 * c), 0.0)
        forces = plane(c) + normal * change
        for t in range(tiles):
            forces_ref[c * tiles + t] = forces[:, t * LANES : (t + 1) * LANES]


def place_kernel(cy, place_ref, count_ref, got_ref, slot_ref, previous_ref, v_ref, owned_ref, message_ref, gram_scratch, forces_ref, held_v, arrived):
    own = place_ref[0]
    sources, tiles = got_ref.shape[0], slot_ref.shape[0] // got_ref.shape[0]
    capacity = previous_ref.shape[1]
    high = capacity // LANES
    base = own * capacity
    fetch = pltpu.make_async_copy(v_ref, held_v, arrived)
    fetch.start()
    corrected(cy, got_ref, tiles, forces_ref)

    def one_source(source, total):
        left, right = [], []
        for t in range(tiles):
            slots = slot_ref[pl.ds(source * tiles + t, 1), :]
            at_row = lax.shift_right_arithmetic(slots - base, 7) == iota((high, LANES), 0)
            right.append((jnp.bitwise_and(slots, LANES - 1) == iota((LANES, LANES), 0)).astype(F32))
            rough, fine = [], []
            for c in range(3):
                value = forces_ref[c * tiles + t, pl.ds(source, 1), :]
                near = value.astype(BF16).astype(F32)
                rough.append(jnp.where(at_row, near, 0.0))
                fine.append(jnp.where(at_row, value - near, 0.0))
            left.append(jnp.concatenate(rough + fine, axis=0))
        left = jnp.concatenate(left, axis=1).astype(BF16)
        right = jnp.concatenate(right, axis=1).astype(BF16)
        return total + lax.dot_general(
            left, right, (((1,), (1,)), ((), ())), preferred_element_type=F32
        )

    total = lax.fori_loop(0, sources, one_source, jnp.zeros((6 * high, LANES), F32), unroll=8)
    owned = total[: 3 * high] + total[3 * high :]
    fetch.wait()
    summed = jnp.zeros((v_ref.shape[1], LANES), F32)
    for c in range(3):
        for h in range(high):
            lanes = slice(h * LANES, (h + 1) * LANES)
            row = owned[c * high + h : c * high + h + 1]
            owned_ref[c : c + 1, lanes] = row
            held = iota((1, LANES), 1) + h * LANES < count_ref[0]
            residual = jnp.where(held, row - previous_ref[c : c + 1, lanes], 0.0)
            summed += held_v[c, :, lanes] * residual
    projection = lax.dot_general(
        jnp.ones((8, LANES), F32), summed, (((1,), (1,)), ((), ())), precision=HIGHEST, preferred_element_type=F32
    )
    gram_rows = gram_scratch.shape[0]
    gram_scratch[...] = jnp.sum(got_ref[:, 5 * tiles + 8 :, :], axis=0)
    chunk = gram_scratch[pl.ds(jnp.minimum(own, gram_rows - 1), 1), :]
    message = jnp.concatenate(
        [
            jnp.where(own < gram_rows, chunk, 0.0),
            projection[:1],
            jnp.zeros((1, LANES - projection.shape[1]), F32),
        ],
        axis=1,
    )
    message_ref[...] = jnp.broadcast_to(message[None], message_ref.shape)


def place(devices, cy, own, counts, got, slots, previous, v):
    columns = v.shape[1]
    return pl.pallas_call(
        functools.partial(place_kernel, cy),
        out_shape=(
            jax.ShapeDtypeStruct(previous.shape, F32),
            jax.ShapeDtypeStruct((devices, 1, 2 * LANES), F32),
        ),
        in_specs=[SMEM, SMEM, VMEM, VMEM, VMEM, ANY],
        out_specs=(VMEM, VMEM),
        scratch_shapes=[
            pltpu.VMEM((columns * columns // LANES, LANES), F32),
            pltpu.VMEM((3 * slots.shape[0] // got.shape[0], got.shape[0], LANES), F32),
            pltpu.VMEM(v.shape, F32),
            pltpu.SemaphoreType.DMA,
        ],
        compiler_params=limit(12),
        name="place",
    )(own, counts, got, slots, previous, v)


def solve_kernel(groups, count_ref, got_ref, owned_ref, w_ref, coupled_ref, held_w, arrived):
    fetch = pltpu.make_async_copy(w_ref, held_w, arrived)
    fetch.start()
    columns, capacity = w_ref.shape[1], w_ref.shape[2]
    gram_rows = columns * columns // LANES
    per_group = got_ref.shape[0] // groups
    tile = got_ref[:gram_rows, 0, :LANES]
    for g in range(1, groups):
        tile += got_ref[g * per_group : g * per_group + gram_rows, 0, :LANES]
    projection = jnp.sum(got_ref[:, 0, LANES:], axis=0, keepdims=True)
    gram = jnp.concatenate([tile[:, j : j + columns] for j in range(0, LANES, columns)], axis=0)
    rows, lanes = iota((columns, LANES), 0), iota((columns, LANES), 1)
    right = jnp.sum(jnp.where(rows == lanes, projection, 0.0), axis=1, keepdims=True)
    system = jnp.concatenate([gram, jnp.zeros((columns, LANES - columns), F32)], axis=1)
    system = jnp.where(lanes == columns, right, system)
    block = 8
    for k in range(0, columns, block):
        pivots = [system[k + i : k + i + 1] for i in range(block)]
        entry = [
            [jnp.broadcast_to(pivots[i][:, k + j : k + j + 1], (1, LANES)) for j in range(block)]
            for i in range(block)
        ]
        for i in range(block):
            inverse = 1.0 / entry[i][i]
            pivots[i] = pivots[i] * inverse
            entry[i] = [part * inverse if j > i else part for j, part in enumerate(entry[i])]
            for m in range(block):
                if m != i:
                    share = entry[m][i]
                    pivots[m] = pivots[m] - share * pivots[i]
                    entry[m] = [
                        part - share * entry[i][j] if j > i else part for j, part in enumerate(entry[m])
                    ]
        rest = system
        for i in range(block):
            rest = rest - system[:, k + i : k + i + 1] * pivots[i]
        for i in range(block):
            rest = jnp.where(rows == k + i, pivots[i], rest)
        system = rest
    coefficient = -system[:, columns : columns + 1]
    fetch.wait()
    for c in range(3):
        for h in range(capacity // LANES):
            at = slice(h * LANES, (h + 1) * LANES)
            update = jnp.sum(held_w[c, :, at] * coefficient, axis=0, keepdims=True)
            held = iota((1, LANES), 1) + h * LANES < count_ref[0]
            coupled_ref[c : c + 1, at] = jnp.where(held, owned_ref[c : c + 1, at] + update, 0.0)


def solve(groups, counts, got, owned, w):
    return pl.pallas_call(
        functools.partial(solve_kernel, groups),
        out_shape=jax.ShapeDtypeStruct(owned.shape, F32),
        in_specs=[SMEM, VMEM, VMEM, ANY],
        out_specs=VMEM,
        scratch_shapes=[pltpu.VMEM(w.shape, F32), pltpu.SemaphoreType.DMA],
        compiler_params=limit(8),
        name="solve",
    )(counts, got, owned, w)


def shifted(here, low, high):
    y, z = iota(here.shape, 0), iota(here.shape, 1)
    before = jnp.where(y == 0, low, rolled(here, 1, 0))
    after = jnp.where(y == here.shape[0] - 1, high, rolled(here, -1, 0))
    left = jnp.where(z == 0, 0.0, rolled(here, 1))
    right = jnp.where(z == here.shape[1] - 1, 0.0, rolled(here, -1))
    return before + after + left + right


CHUNK = 8


def halo_plane(even, first_ref, second_ref, k, above, cy):
    rows = slice(k * cy, (k + 1) * cy)
    return jnp.where(even != above, second_ref[rows], first_ref[rows])


def edge_kernel(
    cy, even_x_ref, even_y_ref, held, first_ref, second_ref, y_first_ref, y_second_ref, to_first_ref, to_second_ref
):
    cx, cz = held.shape[1:]
    even_x, even_y = even_x_ref[0] == 1, even_y_ref[0] == 1
    x, z = iota((cx, cz), 0), iota((cx, cz), 1)
    rows = []
    for side, y in enumerate((0, cy - 1)):
        here, inner, source, diagonal = [held[4 * side + k] for k in range(4)]
        below = halo_plane(even_x, first_ref, second_ref, 0, False, cy)[y : y + 1]
        above = halo_plane(even_x, first_ref, second_ref, 0, True, cy)[y : y + 1]
        total = source + inner + jnp.where(even_y != (side == 1), y_second_ref[...], y_first_ref[...])
        total += jnp.where(x == 0, below, rolled(here, 1, 0)) + jnp.where(x == cx - 1, above, rolled(here, -1, 0))
        total += jnp.where(z == 0, 0.0, rolled(here, 1)) + jnp.where(z == cz - 1, 0.0, rolled(here, -1))
        once = total * (1.0 / (6.0 + diagonal))
        rows.append((once, jnp.concatenate([below, above, jnp.zeros((6, cz), F32)], axis=0)))
    for at, k in ((slice(0, cx), 0), (slice(cx, cx + 8), 1)):
        to_first_ref[at] = jnp.where(even_y, rows[1][k], rows[0][k])
        to_second_ref[at] = jnp.where(even_y, rows[0][k], rows[1][k])


def swept_edges(even_x, even_y, cy, columns, first, second, y_first, y_second):
    cx, cz = columns.shape[1:]
    out = jax.ShapeDtypeStruct((cx + 8, cz), F32)
    return pl.pallas_call(
        functools.partial(edge_kernel, cy),
        out_shape=(out, out),
        in_specs=[SMEM, SMEM] + [VMEM] * 5,
        out_specs=(VMEM, VMEM),
        compiler_params=limit(8),
        name="edges",
    )(even_x, even_y, in_vmem(columns), first, second, y_first, y_second)


def sweeps_kernel(
    even_x_ref, even_y_ref, p_ref, d_ref, g_ref, first_ref, second_ref, y_first_ref, y_second_ref,
    far_first_ref, far_second_ref, out_ref, held_p, held_d, held_g, once_ref, rows_ref, in_sems, out_sems,
):
    cx, cy, cz = p_ref.shape
    steps = cx // CHUNK
    even_x, even_y = even_x_ref[0] == 1, even_y_ref[0] == 1

    def arrive(at):
        planes = pl.ds(at * CHUNK, CHUNK)
        return [
            pltpu.make_async_copy(ref.at[planes], held.at[planes], in_sems.at[k, at])
            for k, (ref, held) in enumerate(((p_ref, held_p), (d_ref, held_d), (g_ref, held_g)))
        ]

    def leave(at):
        planes = pl.ds(at * CHUNK, CHUNK)
        return pltpu.make_async_copy(held_p.at[planes], out_ref.at[planes], out_sems.at[at])

    for at in range(steps):
        for copy in arrive(at):
            copy.start()
    for k, (one, two) in enumerate(((y_first_ref, y_second_ref), (far_first_ref, far_second_ref))):
        rows_ref[2 * k, : one.shape[0]] = jnp.where(even_y, two[...], one[...])
        rows_ref[2 * k + 1, : one.shape[0]] = jnp.where(even_y, one[...], two[...])
    halo = lambda k, above: halo_plane(even_x, first_ref, second_ref, k, above, cy)

    def sweep(before, here, after, source, ratio, low, high):
        return (source + before + after + shifted(here, low, high)) * ratio

    def rows(k, at):
        return [rows_ref[2 * k + side, pl.ds(pl.multiple_of(at * CHUNK, CHUNK), CHUNK), :] for side in range(2)]

    for copy in arrive(0):
        copy.wait()

    def first_chunk(at, carry):
        @pl.when(at + 1 < steps)
        def _():
            for copy in arrive(jnp.minimum(at + 1, steps - 1)):
                copy.wait()

        before, here = carry
        lows, highs = rows(0, at)
        for j in range(CHUNK):
            x = at * CHUNK + j
            after = held_p[jnp.minimum(x + 1, cx - 1)]
            if j == CHUNK - 1:
                after = jnp.where(x == cx - 1, halo(0, True), after)
            ratio = 1.0 / (6.0 + held_g[x])
            once_ref[x] = sweep(before, here, after, held_d[x], ratio, lows[j : j + 1], highs[j : j + 1])
            held_g[x] = ratio
            before, here = here, after
        return before, here

    lax.fori_loop(0, steps, first_chunk, (halo(0, False), held_p[0]))
    ends = [rows_ref[2 + side, cx : cx + 8] for side in range(2)]
    start = sweep(
        halo(1, False), halo(0, False), held_p[0], halo(2, False), halo(3, False), ends[0][:1], ends[1][:1]
    )
    once_ref[cx] = sweep(
        held_p[cx - 1], halo(0, True), halo(1, True), halo(2, True), halo(3, True), ends[0][1:2], ends[1][1:2]
    )

    def second_chunk(at, carry):
        before, here = carry
        lows, highs = rows(1, at)
        for j in range(CHUNK):
            x = at * CHUNK + j
            after = once_ref[x + 1]
            held_p[x] = sweep(before, here, after, held_d[x], held_g[x], lows[j : j + 1], highs[j : j + 1])
            before, here = here, after
        leave(at).start()
        return before, here

    lax.fori_loop(0, steps, second_chunk, (start, once_ref[0]))
    for at in range(steps):
        leave(at).wait()


def both_sweeps(even_x, even_y, p, d, g, *beside):
    cx, cy, cz = p.shape
    return pl.pallas_call(
        sweeps_kernel,
        out_shape=jax.ShapeDtypeStruct(p.shape, F32),
        in_specs=[SMEM, SMEM] + [ANY] * 3 + [VMEM] * 6,
        out_specs=ANY,
        scratch_shapes=[pltpu.VMEM(p.shape, F32)] * 3
        + [
            pltpu.VMEM((cx + 1, cy, cz), F32),
            pltpu.VMEM((4, cx + 8, cz), F32),
            pltpu.SemaphoreType.DMA((3, cx // CHUNK)),
            pltpu.SemaphoreType.DMA((cx // CHUNK,)),
        ],
        compiler_params=limit(20),
        name="sweeps",
    )(even_x, even_y, in_hbm(p), in_hbm(d), in_hbm(g), *beside)


def shards(
    pressure, divergence, diagonal, normals, traction, slot_of, counts, previous, secant_v, secant_w
):
    groups, owners = lax.axis_size("gx"), lax.axis_size("gy")
    cy = pressure.shape[1]
    v = jnp.transpose(secant_v, (1, 0, 2))
    w = jnp.transpose(secant_w, (1, 0, 2))
    own = lax.axis_index("gy").astype(jnp.int32).reshape(1)
    even_x, even_y = [(1 - lax.axis_index(axis) % 2).astype(jnp.int32).reshape(1) for axis in ("gx", "gy")]
    fluid = (even_x, even_y, pressure, divergence, diagonal)
    y_edges = traded(*outer_y_edges(even_y, pressure), "gy")
    faces = traded(*outer_faces(even_x, pressure, divergence, diagonal), "gx")
    planes, columns = slab(pressure, divergence, diagonal)
    y_edges, faces = lax.optimization_barrier((y_edges, faces))
    gram = gram_tile(counts, v)
    block = surface_message(owners, cy, even_x, planes, *faces, normals, traction, gram)
    got = lax.all_to_all(block, "gy", 0, 0, tiled=True)
    far_edges = traded(*swept_edges(even_x, even_y, cy, columns, *faces, *y_edges), "gy")
    owned, message = place(
        groups * owners, cy, own, counts, got, slot_of.reshape(-1, LANES), previous, v
    )
    shared = lax.all_to_all(message, ("gx", "gy"), 0, 0, tiled=True)
    field = both_sweeps(*fluid, *faces, *y_edges, *far_edges)
    coupled = solve(groups, counts, shared, owned, w)
    return (field, coupled)


def solution(mesh):
    placed = (
        P("gx", "gy", None),
        P("gx", "gy", None),
        P("gx", "gy", None),
        P(None, ("gx", "gy")),
        P(None, ("gx", "gy")),
        P("gx", None),
        P(("gx", "gy")),
        P(None, ("gx", "gy")),
        P(None, None, ("gx", "gy")),
        P(None, None, ("gx", "gy")),
    )
    return jax.shard_map(
        shards,
        mesh=mesh,
        in_specs=placed,
        out_specs=(P("gx", "gy", None), P(None, ("gx", "gy"))),
        check_vma=False,
    )
```
